256 devices in a mesh: sec: 4 (over z_hi), area: 16 (over x, z_lo, core), chan: 4 (over y).
Axes of the slice: x: 4, y: 4, z: 8 (z_hi: 4, z_lo: 2; z = z_hi * 2 + z_lo), core: 2. Of those that a mesh axis runs over, the one named last changes fastest.
Arguments:
- features: bfloat16 [8, 64, 4096, 256], P('sec', 'chan', 'area'), may hold values from -6 to 6
- coarse: int32 [2, 8, 128, 8], P(None, 'sec', 'area'), may hold values from -7 to 7
Outputs:
- warped: bfloat16 [8, 64, 4096, 256], P('sec', 'chan', 'area')
- drift_field: float32 [2, 8, 128, 8], P(None, 'sec', 'area')
The draws below stay inside these ranges and needn't reach their ends.
All inputs are finite; a program needn't handle non-finite values.
Results may differ from the reference program's by a relative error of at most 0.00045.
Values may be sent and summed in bfloat16 or wider, within the bound.
A program may use at most 128 MiB of HBM per device.

```python
import math
import jax
import jax.numpy as jnp
from jax import lax

C = 64
TILE = 32
MAXD = 7
R = 1
SMOOTH = 3
W = 256
S = 8
H = 4096
NTY = 128
NTX = 8
HALO = 57


def draw_coarse(key, part):
    key = jax.random.fold_in(key, 11)
    pattern_key, level_key, mask_key, jitter_key, inward_key = jax.random.split(key, 5)
    base_set = jnp.array([1, 1, -1, -1, 0, 0, 0, 0], jnp.int32)
    pattern = jnp.stack([jax.random.permutation(jax.random.fold_in(pattern_key, comp), base_set) for comp in range(2)], 0)
    tile_row = jnp.arange(NTY, dtype=jnp.int32)
    tile_col = jnp.arange(NTX, dtype=jnp.int32)
    block_row = tile_row * 4 // NTY
    block_col = tile_col * 2 // NTX
    first_row = block_row != (tile_row - 1) * 4 // NTY
    first_col = block_col != (tile_col - 1) * 2 // NTX
    anchor = jnp.logical_and(first_row[:, None], first_col[None, :])
    block_index = block_row[:, None] * 2 + block_col[None, :]
    sign_field = pattern[:, block_index]
    field_shape = (2, S, NTY, NTX)
    levels = jax.random.randint(level_key, (2, S, 8), 0 - MAXD, MAXD + 1)
    free_level = levels[:, :, block_index]
    jitter = jax.random.randint(jitter_key, field_shape, -1, 2)
    jitter_mask = jax.random.randint(mask_key, field_shape, 0, 4) == 0
    free_value = jnp.clip(free_level + jnp.where(jitter_mask, jitter, 0), 0 - MAXD, MAXD)
    inward = jnp.logical_and(jax.random.randint(inward_key, field_shape, 0, 16) == 0, jnp.logical_not(anchor)[None, None])
    steady_value = sign_field[:, None] * (MAXD - inward.astype(jnp.int32))
    return jnp.where(sign_field[:, None] != 0, steady_value, free_value).astype(jnp.int32)


def shard_levels(own_key, extent, cuts, low, largest):
    factor_of = 1.0
    for position, parts in cuts:
        steps = jax.random.uniform(jax.random.fold_in(jax.random.fold_in(own_key, 6), position), (parts,), jnp.float32, low / len(cuts), largest / len(cuts))
        factor_of = factor_of * jnp.repeat(jnp.exp(steps), extent[position] // parts).reshape((-1,) + (1,) * (len(extent) - 1 - position))
    return factor_of


def normal_values(rng, shape, deviation, most, shards=(), kind=jnp.bfloat16):
    factor_of = shard_levels(rng, shape, shards, -0.22, 0.18) if shards else 1.0
    drawn = jax.random.normal(rng, shape, jnp.float32) * deviation * factor_of
    return jnp.minimum(jnp.maximum(drawn, -most), most).astype(kind)


def setup_inputs(seed: int = 0) -> dict:
    keys = jax.random.split(jax.random.key(seed), 3)
    features = normal_values(keys[0], (S, C, H, W), 1.0, 6.0, ((0, 4), (1, 4), (2, 16)))
    coarse = draw_coarse(jax.random.fold_in(keys[2], 71), 0)
    return {"features": features, "coarse": coarse}


def index_tuple(values):
    return tuple((jnp.asarray(value).astype(jnp.int32) for value in values))

def centroid(scores):
    span_side = 2 * R + 1
    offsets = jnp.arange(span_side * span_side, dtype=jnp.int32)
    row_offset = (offsets // span_side - R).astype(jnp.float32)
    col_offset = (offsets % span_side - R).astype(jnp.float32)
    weights = jax.nn.sigmoid(scores)
    weight_total = lax.optimization_barrier(jnp.sum(weights, axis=-1))
    return jnp.stack([lax.optimization_barrier(jnp.sum(weights * row_offset, axis=-1)) / weight_total, lax.optimization_barrier(jnp.sum(weights * col_offset, axis=-1)) / weight_total], 0)

def score_tiles(features, reference_pad, coarse):
    sections, channels, row_count, col_count = features.shape
    rows_tiles = row_count // TILE
    cols_tiles = col_count // TILE
    per_section = rows_tiles * cols_tiles
    span_side = 2 * R + 1
    reach_rows = MAXD + R

    def one_tile(tile_index):
        section = tile_index // per_section
        remainder = tile_index % per_section
        tile_row = remainder // cols_tiles
        tile_col = remainder % cols_tiles
        top_row = tile_row * TILE
        left_col = tile_col * TILE
        moving = lax.dynamic_slice(features, index_tuple((section, 0, top_row, left_col)), (1, channels, TILE, TILE))[0].astype(jnp.float32)
        start_row = top_row + coarse[0, section, tile_row, tile_col] + reach_rows - R
        start_col = left_col + coarse[1, section, tile_row, tile_col] + reach_rows - R
        window = lax.dynamic_slice(reference_pad, index_tuple((section, 0, start_row, start_col)), (1, channels, TILE + 2 * R, TILE + 2 * R))[0].astype(jnp.float32)
        partials = [jnp.sum(moving * window[:, i:i + TILE, j:j + TILE]) for i in range(span_side) for j in range(span_side)]
        return jnp.stack(partials)
    indices = jnp.arange(sections * per_section, dtype=jnp.int32)
    return lax.map(one_tile, indices).reshape(sections, rows_tiles, cols_tiles, span_side * span_side)

def warp_tiles(padded, drift_field, margin, row_count, col_count):
    sections, channels = (padded.shape[0], padded.shape[1])
    rows_tiles = row_count // TILE
    cols_tiles = col_count // TILE
    per_section = rows_tiles * cols_tiles

    def one_tile(tile_index):
        section = tile_index // per_section
        remainder = tile_index % per_section
        tile_row = remainder // cols_tiles
        tile_col = remainder % cols_tiles
        shift_down = drift_field[0, section, tile_row, tile_col]
        shift_across = drift_field[1, section, tile_row, tile_col]
        floor_row = jnp.floor(shift_down)
        floor_col = jnp.floor(shift_across)
        frac_row = shift_down - floor_row
        frac_col = shift_across - floor_col
        start_row = tile_row * TILE + margin + floor_row.astype(jnp.int32)
        start_col = tile_col * TILE + margin + floor_col.astype(jnp.int32)
        window = lax.dynamic_slice(padded, index_tuple((section, 0, start_row, start_col)), (1, channels, TILE + 1, TILE + 1))[0].astype(jnp.float32)
        upper_mix = (1 - frac_col) * window[:, :TILE, :TILE] + frac_col * window[:, :TILE, 1:]
        lower_mix = (1 - frac_col) * window[:, 1:, :TILE] + frac_col * window[:, 1:, 1:]
        return ((1 - frac_row) * upper_mix + frac_row * lower_mix).astype(jnp.bfloat16)
    indices = jnp.arange(sections * per_section, dtype=jnp.int32)
    warped_tiles = lax.map(one_tile, indices)
    warped_tiles = warped_tiles.reshape(sections, rows_tiles, cols_tiles, channels, TILE, TILE)
    return warped_tiles.transpose(0, 3, 1, 4, 2, 5).reshape(sections, channels, row_count, col_count)

def smooth_field(drift_field):
    extended = jnp.pad(drift_field, ((0, 0), (0, 0), (1, 1), (1, 1)))
    neighbours = extended[:, :, :-2, 1:-1] + extended[:, :, 2:, 1:-1] + extended[:, :, 1:-1, :-2] + extended[:, :, 1:-1, 2:]
    in_grid = jnp.pad(jnp.ones(drift_field.shape[2:], jnp.float32), 1)
    counts = in_grid[:-2, 1:-1] + in_grid[2:, 1:-1] + in_grid[1:-1, :-2] + in_grid[1:-1, 2:]
    return (drift_field + neighbours) / (1.0 + counts)

def reference(features, coarse):
    sections, channels, row_count, col_count = features.shape
    reach_rows = MAXD + R
    prior = jnp.concatenate([jnp.zeros_like(features[:1]), features[:-1]], 0)
    reference_pad = jnp.pad(prior, ((0, 0), (0, 0), (reach_rows, reach_rows), (reach_rows, reach_rows)))
    scores = score_tiles(features, reference_pad, coarse) * (1.0 / math.sqrt(C * TILE * TILE))
    fine = centroid(scores)
    keep = (jnp.arange(sections, dtype=jnp.int32) >= 1).astype(jnp.float32)
    pair_field = (coarse.astype(jnp.float32) + fine) * keep[None, :, None, None]
    drift_field = jnp.cumsum(pair_field, axis=1)
    for sweep in range(SMOOTH):
        drift_field = smooth_field(drift_field)
    source = jnp.pad(features, ((0, 0), (0, 0), (HALO, HALO), (HALO, HALO)))
    warped = warp_tiles(source, drift_field, HALO, row_count, col_count)
    return (warped, drift_field)
```

```python
import math

import jax
import jax.numpy as jnp
from jax import lax
from jax.experimental import pallas as pl
from jax.experimental.pallas import tpu as pltpu

from jax.sharding import PartitionSpec as P

C = 64
TILE = 32
MAXD = 7
R = 1
SMOOTH = 3
HALO = 64
BF = jnp.bfloat16
F32 = jnp.float32


def lane_pick(scalars, lanes_tile):
    out = jnp.full(lanes_tile.shape, scalars[0])
    for t in range(1, len(scalars)):
        out = jnp.where(lanes_tile == t, scalars[t], out)
    return out


def score_row(f_rows, p_rows, coarse_row, coarse_col, left, right, count):
    src = lax.broadcasted_iota(jnp.int32, (256, 128), 0)
    lane = lax.broadcasted_iota(jnp.int32, (1, 128), 1)
    lane_tile = lane // TILE
    shifts = []
    for h in range(2):
        col = lane + 128 * h + lane_pick([coarse_col[4 * h + t] for t in range(4)], lane_tile)
        rel = src - col
        for b in (-1, 0, 1):
            shifts.append(jnp.where(rel == b, 1.0, 0.0).astype(BF))
    shifted = jnp.concatenate(shifts, 1)
    window = p_rows()
    for c0 in range(0, count, 4):
        moved = lax.dot_general(
            window[c0 * 64 : (c0 + 4) * 64], shifted, (((1,), (0,)), ((), ())), preferred_element_type=F32
        ).astype(BF)
        for c in range(c0, c0 + 4):
            for h in range(2):
                for b in range(3):
                    right[h, 64 * b : 64 * b + 64, 128 * c : 128 * c + 128] = moved[
                        64 * (c - c0) : 64 * (c - c0) + 64, 384 * h + 128 * b : 384 * h + 128 * b + 128
                    ]
    tile_masks = [lax.broadcasted_iota(jnp.int32, (TILE, 128), 1) // TILE == t for t in range(4)]
    for c in range(count):
        strip = f_rows(c)
        for h in range(2):
            part = strip[:, 128 * h : 128 * h + 128]
            for t in range(4):
                left[h, TILE * t : TILE * t + TILE, 128 * c : 128 * c + 128] = jnp.where(
                    tile_masks[t], part, jnp.zeros_like(part)
                )
    row = lax.broadcasted_iota(jnp.int32, (128, 192), 0)
    col = lax.broadcasted_iota(jnp.int32, (128, 192), 1)
    base = col % 64 - 16 - row % TILE
    row_tile = lax.broadcasted_iota(jnp.int32, (128, 1), 0) // TILE
    out = [[], [], []]
    for h in range(2):
        gram = lax.dot_general(
            left[h, :, : count * 128],
            right[h, :, : count * 128],
            (((1,), (1,)), ((), ())),
            preferred_element_type=F32,
        )
        rel = base - lane_pick([coarse_row[4 * h + t] for t in range(4)], row_tile)
        for a in range(3):
            kept = jnp.where(rel == a - 1, gram, 0.0)
            out[a].append(jnp.sum(kept.reshape(4, TILE, 192), axis=1))
    return [jnp.concatenate(o, 0) for o in out]


def score_kernel(coarse, f_ref, p0_ref, p1_ref, out_ref, left, right, acc):
    for s, p_ref in ((0, p0_ref), (1, p1_ref)):

        def step(ty, _):
            crow = [coarse[0, s * 64 + ty * 8 + t] for t in range(8)]
            ccol = [coarse[1, s * 64 + ty * 8 + t] for t in range(8)]
            top = pl.multiple_of(ty * TILE, TILE)
            blocks = score_row(
                lambda c: f_ref[s, c, pl.ds(top, TILE), :],
                lambda: p_ref[:, pl.ds(top, 64), :].reshape(16 * 64, 256),
                crow,
                ccol,
                left,
                right,
                16,
            )
            for a in range(3):
                acc[a, pl.ds(pl.multiple_of(s * 64 + ty * 8, 8), 8), :] = blocks[a]
            return 0

        lax.fori_loop(0, 8, step, 0)
    seg = lax.broadcasted_iota(jnp.int32, (8, 192), 1) // 64
    pick = (seg == lax.broadcasted_iota(jnp.int32, (8, 192), 0)).astype(F32)
    for a in range(3):
        out_ref[a] = lax.dot_general(
            pick, acc[a], (((1,), (1,)), ((), ())), precision=lax.Precision.HIGHEST, preferred_element_type=F32
        )


def scores_local(coarse, features, prior0, prior1):
    vm = pl.BlockSpec(memory_space=pltpu.VMEM)
    return pl.pallas_call(
        score_kernel,
        out_shape=jax.ShapeDtypeStruct((3, 8, 128), F32),
        in_specs=[pl.BlockSpec(memory_space=pltpu.SMEM), vm, vm, vm],
        out_specs=vm,
        scratch_shapes=[
            pltpu.VMEM((2, 128, 2048), BF),
            pltpu.VMEM((2, 192, 2048), BF),
            pltpu.VMEM((3, 128, 192), F32),
        ],
        compiler_params=pltpu.CompilerParams(vmem_limit_bytes=56 * 2**20),
        name="scores",
    )(coarse, features, prior0, prior1)


def warp_kernel(whole, frac, src, out_ref, held, rows, sems):
    step = pl.program_id(0)
    s = step // 8
    ty = step % 8

    def load(k):
        return pltpu.make_async_copy(src.at[k], held.at[k], sems.at[k])

    @pl.when(step == 0)
    def _():
        load(0).start()
        load(1).start()
        load(0).wait()

    @pl.when(step == 8)
    def _():
        load(1).wait()

    lane = lax.broadcasted_iota(jnp.int32, (1, 128), 1)
    lane_tile = lane // TILE
    src_col = lax.broadcasted_iota(jnp.int32, (256, 128), 0)
    base = HALO + TILE * ty
    for h in range(2):
        at = step * 8 + 4 * h
        fl_row = [whole[0, at + t] for t in range(4)]
        fl_col = [whole[1, at + t] for t in range(4)]
        fr_row = lane_pick([frac[0, at + t] for t in range(4)], lane_tile)
        fr_col = lane_pick([frac[1, at + t] for t in range(4)], lane_tile)
        low = jnp.minimum(jnp.minimum(fl_row[0], fl_row[1]), jnp.minimum(fl_row[2], fl_row[3]))
        high = jnp.maximum(jnp.maximum(fl_row[0], fl_row[1]), jnp.maximum(fl_row[2], fl_row[3]))
        start = jnp.minimum((base + low) // 16 * 16, 2 * HALO + 256 - 48)
        chunks = (base + high + TILE + 1 - start + 15) // 16
        rel = src_col - (lane + 128 * h + lane_pick(fl_col, lane_tile))
        weight = jnp.where(rel == 0, 1.0 - fr_col, jnp.where(rel == 1, fr_col, 0.0))
        coarse_part = weight.astype(BF)
        fine_part = (weight - coarse_part.astype(F32)).astype(BF)
        mixer = jnp.concatenate([coarse_part, fine_part], 1)

        def chunk(r, _):
            at_row = pl.multiple_of(start + 16 * r, 16)
            block = held[s, :, pl.ds(at_row, 16), :].reshape(256, 256)
            mixed = jnp.dot(block, mixer, preferred_element_type=F32)
            mixed = mixed[:, :128] + mixed[:, 128:]
            rows[:, pl.ds(pl.multiple_of(16 * r, 16), 16), :] = mixed.reshape(16, 16, 128)
            return 0

        for r in range(3):
            chunk(r, 0)
        lax.fori_loop(3, chunks, chunk, 0)
        offs = [base + fl_row[t] - start for t in range(4)]
        for c in range(16):
            upper = rows[c, pl.ds(offs[0], TILE), :]
            lower = rows[c, pl.ds(offs[0] + 1, TILE), :]
            for t in range(1, 4):
                mine = lane_tile == t
                upper = jnp.where(mine, rows[c, pl.ds(offs[t], TILE), :], upper)
                lower = jnp.where(mine, rows[c, pl.ds(offs[t] + 1, TILE), :], lower)
            out_ref[0, c, :, 128 * h : 128 * h + 128] = ((1.0 - fr_row) * upper + fr_row * lower).astype(BF)


def warp_local(whole, frac, source):
    sm = pl.BlockSpec(memory_space=pltpu.SMEM)
    return pl.pallas_call(
        warp_kernel,
        grid=(16,),
        out_shape=jax.ShapeDtypeStruct((2, 16, 256, 256), BF),
        in_specs=[sm, sm, pl.BlockSpec(memory_space=pl.ANY)],
        out_specs=pl.BlockSpec((1, 16, TILE, 256), lambda g: (g // 8, 0, g % 8, 0)),
        scratch_shapes=[
            pltpu.VMEM((2, 16, 2 * HALO + 256, 256), BF),
            pltpu.VMEM((16, 176, 128), F32),
            pltpu.SemaphoreType.DMA((2,)),
        ],
        compiler_params=pltpu.CompilerParams(vmem_limit_bytes=56 * 2**20),
        name="warp",
    )(whole, frac, source)


def padded_2(cells, sides, width):
    for axis, dim in sides:
        count = lax.axis_size(axis)
        ends = count - 1
        head = lax.slice_in_dim(cells, 0, width, axis=dim)
        tail = lax.slice_in_dim(cells, cells.shape[dim] - width, cells.shape[dim], axis=dim)
        cells = jnp.concatenate(
            [
                lax.ppermute(tail, axis, [(i, (i + 1) % count) for i in range(ends)]),
                cells,
                lax.ppermute(head, axis, [((i + 1) % count, i) for i in range(ends)]),
            ],
            axis=dim,
        )
    return cells


def shifted(shard, axis, by):
    devices = lax.axis_size(axis)
    pairs = [(i, i + by) for i in range(devices) if 0 <= i + by < devices]
    return lax.ppermute(shard, axis, pairs)


def prefix(value, axis, join, neutral):
    count, mine = (lax.axis_size(axis), lax.axis_index(axis))
    pieces = lax.all_gather(value, axis)
    total = jnp.full_like(value, 0) + jnp.asarray(neutral, value.dtype)

    def step(position, total):
        longer = join(total, pieces[position])
        return jnp.where(position < mine, longer, total)

    return lax.fori_loop(0, count - 1, step, total)


def index_tuple(values):
    return tuple((jnp.asarray(value).astype(jnp.int32) for value in values))


def combine_add(earlier, later):
    return earlier + later


def centroid(scores):
    span_side = 2 * R + 1
    offsets = jnp.arange(span_side * span_side, dtype=jnp.int32)
    row_offset = (offsets // span_side - R).astype(jnp.float32)
    col_offset = (offsets % span_side - R).astype(jnp.float32)
    weights = jax.nn.sigmoid(scores)
    weight_total = jnp.sum(weights, axis=-1)
    return jnp.stack(
        [
            jnp.sum(weights * row_offset, axis=-1) / weight_total,
            jnp.sum(weights * col_offset, axis=-1) / weight_total,
        ],
        0,
    )


def smooth_field(drift_field, counts):
    extended = padded_2(drift_field, (("area", 2),), 1)
    extended = jnp.pad(extended, ((0, 0), (0, 0), (0, 0), (1, 1)))
    neighbours = (
        extended[:, :, :-2, 1:-1]
        + extended[:, :, 2:, 1:-1]
        + extended[:, :, 1:-1, :-2]
        + extended[:, :, 1:-1, 2:]
    )
    return (drift_field + neighbours) / (1.0 + counts)


def local(features, coarse):
    sections, channels, row_count, col_count = features.shape
    own = padded_2(features, (("area", 2),), HALO)
    prior = shifted(own[1, :, HALO - 16 : HALO + 272], "sec", 1)
    flat_coarse = coarse.reshape(2, 128)
    sums = scores_local(flat_coarse, features, prior, own[0, :, HALO - 16 : HALO + 272])
    partial_scores = sums[:, :3].reshape(9, 2, 8, 8).transpose(1, 2, 3, 0)
    score_scale = 1.0 / math.sqrt(C * TILE * TILE)
    scores = lax.psum(partial_scores, "chan") * score_scale
    fine = centroid(scores)
    section_index = lax.axis_index("sec") * sections + jnp.arange(sections, dtype=jnp.int32)
    keep = (section_index >= 1).astype(jnp.float32)
    pair_field = (coarse.astype(jnp.float32) + fine) * keep[None, :, None, None]
    local_sum = jnp.cumsum(pair_field, axis=1)
    device_total = local_sum[:, -1]
    earlier = prefix(device_total, "sec", combine_add, jnp.zeros_like(device_total))
    drift_field = local_sum + earlier[:, None]
    rows_tiles = row_count // TILE
    cols_tiles = col_count // TILE
    total_rows = rows_tiles * lax.axis_size("area")
    global_row = lax.axis_index("area") * rows_tiles + jnp.arange(rows_tiles, dtype=jnp.int32)
    local_col = jnp.arange(cols_tiles, dtype=jnp.int32)
    vertical = (global_row > 0).astype(jnp.float32) + (global_row < total_rows - 1).astype(
        jnp.float32
    )
    sideways = (local_col > 0).astype(jnp.float32) + (local_col < cols_tiles - 1).astype(
        jnp.float32
    )
    counts = vertical[:, None] + sideways[None, :]
    for sweep in range(SMOOTH):
        drift_field = smooth_field(drift_field, counts)
    floors = jnp.floor(drift_field)
    warped = warp_local(
        floors.astype(jnp.int32).reshape(2, 128), (drift_field - floors).reshape(2, 128), own
    )
    return (warped, drift_field)


def solution(mesh):
    placed = (P("sec", "chan", "area", None), P(None, "sec", "area", None))
    return jax.shard_map(
        local,
        mesh=mesh,
        in_specs=placed,
        out_specs=(P("sec", "chan", "area", None), P(None, "sec", "area", None)),
        check_vma=False,
    )
```

```python
import functools
import math

import jax
import jax.numpy as jnp
from jax import lax
from jax.experimental import pallas as pl
from jax.experimental.pallas import tpu as pltpu
from jax.sharding import PartitionSpec as P

C = 64
TILE = 32
MAXD = 7
R = 1
SMOOTH = 3
HALO = 64
BF = jnp.bfloat16
F32 = jnp.float32


def lane_pick(scalars, lanes_tile):
    out = jnp.full(lanes_tile.shape, scalars[0])
    for t in range(1, len(scalars)):
        out = jnp.where(lanes_tile == t, scalars[t], out)
    return out


NEAR = 16
WINDOW = 3


def score_rows(f_rows, window, coarse_row, coarse_col, left, right, count):
    src = lax.broadcasted_iota(jnp.int32, (256, 128), 0)
    lane = lax.broadcasted_iota(jnp.int32, (1, 128), 1)
    lane_tile = lane // TILE
    shifts = []
    for h in range(2):
        col = lane + 128 * h + lane_pick([coarse_col[4 * h + t] for t in range(4)], lane_tile)
        rel = src - col
        for b in (-1, 0, 1):
            shifts.append(jnp.where(rel == b, 1.0, 0.0).astype(BF))
    shifted = jnp.concatenate(shifts, 1)
    for c0 in range(0, count, 4):
        moved = lax.dot_general(
            window(c0), shifted, (((1,), (0,)), ((), ())), preferred_element_type=F32
        ).astype(BF)
        for c in range(4):
            for h in range(2):
                for b in range(3):
                    right[h, 64 * b : 64 * b + 64, 128 * (c0 + c) : 128 * (c0 + c) + 128] = moved[
                        64 * c : 64 * c + 64, 384 * h + 128 * b : 384 * h + 128 * b + 128
                    ]
    tile_masks = [lax.broadcasted_iota(jnp.int32, (TILE, 128), 1) // TILE == t for t in range(4)]
    for c in range(count):
        strip = f_rows(c)
        for h in range(2):
            part = strip[:, 128 * h : 128 * h + 128]
            for t in range(4):
                left[h, TILE * t : TILE * t + TILE, 128 * c : 128 * c + 128] = jnp.where(
                    tile_masks[t], part, jnp.zeros_like(part)
                )
    row = lax.broadcasted_iota(jnp.int32, (128, 192), 0)
    col = lax.broadcasted_iota(jnp.int32, (128, 192), 1)
    base = col % 64 - NEAR - row % TILE
    row_tile = lax.broadcasted_iota(jnp.int32, (128, 1), 0) // TILE
    out = [[], [], []]
    for h in range(2):
        gram = lax.dot_general(
            left[h, :, : count * 128],
            right[h, :, : count * 128],
            (((1,), (1,)), ((), ())),
            preferred_element_type=F32,
        )
        rel = base - lane_pick([coarse_row[4 * h + t] for t in range(4)], row_tile)
        for a in range(3):
            kept = jnp.where(rel == a - 1, gram, 0.0)
            out[a].append(jnp.sum(kept.reshape(4, TILE, 192), axis=1))
    return [jnp.concatenate(o, 0) for o in out]


def gather_offsets(acc):
    total = jnp.zeros((16, 128), F32)
    seg = lax.broadcasted_iota(jnp.int32, (16, 192), 1) // 64
    row = lax.broadcasted_iota(jnp.int32, (16, 192), 0)
    for a in range(3):
        pick = (row == seg + 3 * a).astype(F32)
        total = total + lax.dot_general(
            pick, acc[a], (((1,), (1,)), ((), ())), precision=lax.Precision.HIGHEST, preferred_element_type=F32
        )
    return total


def drift_kernel(
    devices, cs, cv, feat,
    field_out, whole_out, frac_out, top_out, bottom_out,
    own, prior, later, later_coarse, later_cs, left, right, acc, acc_later,
    q_send, b_send, q_slots, b_slots, e_send, e_slots,
    load_sem, near_s, near_r, far_s, far_r, edge_s, edge_r, cc_s, cc_r, cc_l,
    a_s, a_r, b_s, b_r, d_s, d_r, g_s, g_r, e_s, e_r, keep_sem,
):
    secs, areas, chans = devices
    k, i, j = (lax.axis_index(name) for name in ("sec", "area", "chan"))
    MESH = pl.DeviceIdType.MESH

    def at(sec, area, chan):
        return {"sec": sec, "area": area, "chan": chan}

    def remote(src, dst, send, recv, target):
        return pltpu.make_async_remote_copy(
            src_ref=src, dst_ref=dst, send_sem=send, recv_sem=recv, device_id=target, device_id_type=MESH
        )

    nxt, prv = lax.rem(k + 1, secs), lax.rem(k + secs - 1, secs)
    down, up = lax.rem(i + 1, areas), lax.rem(i + areas - 1, areas)
    has_next, has_prev = k < secs - 1, k > 0
    has_down, has_up = i < areas - 1, i > 0

    loads = [
        pltpu.make_async_copy(feat.at[s], own.at[s, :, pl.ds(NEAR, 256), :], load_sem.at[s]) for s in range(2)
    ]
    for load in loads:
        load.start()

    barrier = pltpu.get_barrier_semaphore()
    for other in range(secs):
        for side, there in ((-1, has_up), (0, True), (1, has_down)):
            fits = jnp.logical_and(there, jnp.logical_or(side != 0, k != other))

            @pl.when(fits)
            def _():
                pl.semaphore_signal(barrier, inc=1, device_id=at(other, i + side, j), device_id_type=MESH)

    for step, there in ((-1, has_prev), (0, True), (1, has_next)):
        for turn in range(1, chans):

            @pl.when(there)
            def _():
                pl.semaphore_signal(
                    barrier, inc=1, device_id=at(k + step, i, lax.rem(j + turn, chans)), device_id_type=MESH
                )

    one = lambda flag: jnp.where(flag, 1, 0)
    pl.semaphore_wait(
        barrier,
        secs * (1 + one(has_up) + one(has_down)) - 1 + (chans - 1) * (1 + one(has_prev) + one(has_next)),
    )

    near_down = remote(
        feat.at[:, :, pl.ds(256 - NEAR, NEAR), :], own.at[:, :, pl.ds(0, NEAR), :], near_s.at[0], near_r.at[0], at(k, down, j)
    )
    near_up = remote(
        feat.at[:, :, pl.ds(0, NEAR), :], own.at[:, :, pl.ds(NEAR + 256, NEAR), :], near_s.at[1], near_r.at[1], at(k, up, j)
    )
    edge_down = remote(
        feat.at[1, pl.ds(0, 8), pl.ds(256 - NEAR, NEAR), :], prior.at[:, pl.ds(0, NEAR), :], edge_s.at[0], edge_r.at[0], at(nxt, down, j)
    )
    edge_up = remote(
        feat.at[1, pl.ds(0, 8), pl.ds(0, NEAR), :], prior.at[:, pl.ds(NEAR + 256, NEAR), :], edge_s.at[1], edge_r.at[1], at(nxt, up, j)
    )
    coarse_back = remote(cv, later_coarse, cc_s, cc_r, at(prv, i, j))

    def far_down(r):
        rows = HALO - 16 * (r + 1)
        return remote(
            feat.at[:, :, pl.ds(240 - 16 * r, 16), :], top_out.at[:, :, pl.ds(rows, 16), :], far_s.at[0, r], far_r.at[0, r], at(k, down, j)
        )

    def far_up(r):
        return remote(
            feat.at[:, :, pl.ds(16 * r, 16), :], bottom_out.at[:, :, pl.ds(16 * r, 16), :], far_s.at[1, r], far_r.at[1, r], at(k, up, j)
        )

    def ahead(c):
        return remote(
            feat.at[1, pl.ds(0, 8), pl.ds(pl.multiple_of(TILE * c, TILE), TILE), :],
            prior.at[:, pl.ds(pl.multiple_of(NEAR + TILE * c, NEAR), TILE), :],
            a_s.at[c], a_r.at[c], at(nxt, i, j),
        )

    def behind(c):
        return remote(
            feat.at[0, pl.ds(8, 8), pl.ds(pl.multiple_of(TILE * c, TILE), TILE), :],
            later.at[:, pl.ds(pl.multiple_of(TILE * c, TILE), TILE), :],
            b_s.at[c], b_r.at[c], at(prv, i, j),
        )

    def start_parts(c):
        @pl.when(has_next)
        def _():
            ahead(c).start()

        @pl.when(has_prev)
        def _():
            behind(c).start()

    def start_far():
        for r in range(1, 4):

            @pl.when(jnp.logical_and(has_down, k >= r))
            def _():
                far_down(r).start()

            @pl.when(jnp.logical_and(has_up, k >= r))
            def _():
                far_up(r).start()

    @pl.when(has_down)
    def _():
        near_down.start()

    @pl.when(has_up)
    def _():
        near_up.start()

    @pl.when(has_prev)
    def _():
        coarse_back.start()

    @pl.when(jnp.logical_and(has_next, has_down))
    def _():
        edge_down.start()

    @pl.when(jnp.logical_and(has_next, has_up))
    def _():
        edge_up.start()

    for c in range(WINDOW):
        start_parts(c)

    @pl.when(jnp.logical_not(has_next))
    def _():
        start_far()

    @pl.when(jnp.logical_not(has_up))
    def _():
        own[:, :, pl.ds(0, NEAR), :] = jnp.zeros((2, 16, NEAR, 256), BF)
        prior[:, pl.ds(0, NEAR), :] = jnp.zeros((8, NEAR, 256), BF)

    @pl.when(jnp.logical_not(has_down))
    def _():
        own[:, :, pl.ds(NEAR + 256, NEAR), :] = jnp.zeros((2, 16, NEAR, 256), BF)
        prior[:, pl.ds(NEAR + 256, NEAR), :] = jnp.zeros((8, NEAR, 256), BF)

    acc[...] = jnp.zeros_like(acc)
    acc_later[...] = jnp.zeros_like(acc_later)
    for load in loads:
        load.wait()

    keep_top = pltpu.make_async_copy(
        own.at[:, :, pl.ds(0, NEAR), :], top_out.at[:, :, pl.ds(HALO - NEAR, NEAR), :], keep_sem.at[0]
    )
    keep_bottom = pltpu.make_async_copy(
        own.at[:, :, pl.ds(NEAR + 256, NEAR), :], bottom_out.at[:, :, pl.ds(0, NEAR), :], keep_sem.at[1]
    )

    @pl.when(has_up)
    def _():
        near_down.wait_recv()

    @pl.when(has_down)
    def _():
        near_up.wait_recv()

    keep_top.start()
    keep_bottom.start()

    def local_row(ty, _):
        top = pl.multiple_of(ty * TILE, TILE)
        blocks = score_rows(
            lambda c: own[1, c, pl.ds(pl.multiple_of(top + NEAR, NEAR), TILE), :],
            lambda c: own[0, c : c + 4, pl.ds(top, 64), :].reshape(256, 256),
            [cs[0, 64 + ty * 8 + t] for t in range(8)],
            [cs[1, 64 + ty * 8 + t] for t in range(8)],
            left, right, 16,
        )
        for a in range(3):
            acc[a, pl.ds(pl.multiple_of(64 + ty * 8, 8), 8), :] = blocks[a]
        return 0

    lax.fori_loop(0, 8, local_row, 0)

    coarse_local = pltpu.make_async_copy(later_coarse, later_cs, cc_l)

    @pl.when(has_next)
    def _():
        coarse_back.wait_recv()
        coarse_local.start()
        coarse_local.wait()

    @pl.when(has_prev)
    def _():
        ahead(0).wait_recv()

        @pl.when(has_up)
        def _():
            edge_down.wait_recv()

        @pl.when(has_down)
        def _():
            edge_up.wait_recv()

    def remote_row(ty, _):
        top = pl.multiple_of(ty * TILE, TILE)

        @pl.when(has_prev)
        def _():
            @pl.when(ty < 7)
            def _():
                ahead(ty + 1).wait_recv()

            behind(ty).wait_send()

        @pl.when(has_next)
        def _():
            behind(ty).wait_recv()
            ahead(ty).wait_send()

        @pl.when(ty + WINDOW < 8)
        def _():
            start_parts(ty + WINDOW)

        @pl.when(has_prev)
        def _():
            blocks = score_rows(
                lambda c: own[0, c, pl.ds(pl.multiple_of(top + NEAR, NEAR), TILE), :],
                lambda c: prior[c : c + 4, pl.ds(top, 64), :].reshape(256, 256),
                [cs[0, ty * 8 + t] for t in range(8)],
                [cs[1, ty * 8 + t] for t in range(8)],
                left, right, 8,
            )
            for a in range(3):
                acc[a, pl.ds(pl.multiple_of(ty * 8, 8), 8), :] = blocks[a]

        @pl.when(has_next)
        def _():
            blocks = score_rows(
                lambda c: later[c, pl.ds(top, TILE), :],
                lambda c: own[1, 8 + c : 12 + c, pl.ds(top, 64), :].reshape(256, 256),
                [later_cs[0, ty * 8 + t] for t in range(8)],
                [later_cs[1, ty * 8 + t] for t in range(8)],
                left, right, 8,
            )
            for a in range(3):
                acc_later[a, pl.ds(pl.multiple_of(ty * 8, 8), 8), :] = blocks[a]

        return 0

    lax.fori_loop(0, 8, remote_row, 0)

    mine = gather_offsets(acc)
    q_send[...] = mine
    q_slots[j] = mine
    b_send[...] = gather_offsets(acc_later)

    def share(turn):
        return remote(q_send, q_slots.at[j], d_s.at[turn], d_r.at[turn], at(k, i, lax.rem(j + turn, chans)))

    def give(turn):
        return remote(b_send, b_slots.at[j], g_s.at[turn], g_r.at[turn], at(nxt, i, lax.rem(j + turn, chans)))

    for turn in range(chans):

        @pl.when(has_next)
        def _():
            give(turn).start()

        if turn:
            share(turn).start()

    @pl.when(has_next)
    def _():
        start_far()

    for turn in range(chans):
        if turn:
            share(turn).wait_recv()

        @pl.when(has_prev)
        def _():
            give(turn).wait_recv()

    total = jnp.zeros((16, 128), F32)
    for chan in range(chans):
        total = total + q_slots[chan]
    for chan in range(chans):
        total = total + jnp.where(has_prev, b_slots[chan], 0.0)
    scores = total * (1.0 / math.sqrt(C * TILE * TILE))
    row = lax.broadcasted_iota(jnp.int32, (16, 128), 0)
    weights = jnp.where(row < 9, 1.0 / (1.0 + jnp.exp(-scores)), 0.0)
    weight_total = jnp.sum(weights, axis=0, keepdims=True)
    fine_row = jnp.sum(weights * (row // 3 - 1).astype(F32), axis=0, keepdims=True) / weight_total
    fine_col = jnp.sum(weights * (row % 3 - 1).astype(F32), axis=0, keepdims=True) / weight_total
    lane = lax.broadcasted_iota(jnp.int32, (8, 128), 1)
    comp = lax.broadcasted_iota(jnp.int32, (8, 128), 0)
    moved = cv[...].astype(F32)
    pair = jnp.where(comp == 0, moved[0:1] + fine_row, moved[1:2] + fine_col)
    pair = jnp.where(jnp.logical_and(comp < 2, jnp.logical_or(has_prev, lane >= 64)), pair, 0.0)
    e_send[...] = pair
    e_slots[k * 3 + 1] = pair

    def tell(ahead_by, side):
        slot = k * 3 + 1 - side
        return remote(
            e_send, e_slots.at[slot], e_s.at[ahead_by, side + 1], e_r.at[slot],
            at(lax.rem(k + ahead_by, secs), lax.rem(i + side + areas, areas), j),
        )

    sides = ((-1, has_up), (0, True), (1, has_down))
    messages = [
        (ahead_by, side, jnp.logical_and(there, k + ahead_by < secs))
        for ahead_by in range(secs)
        for side, there in sides
        if ahead_by or side
    ]
    for ahead_by, side, fits in messages:

        @pl.when(fits)
        def _():
            tell(ahead_by, side).start()

    def hear(sec, side):
        return remote(
            e_send, e_slots.at[sec * 3 + 1 + side], e_s.at[0, 0], e_r.at[sec * 3 + 1 + side], at(prv, i, j)
        )

    for sec in range(secs):
        for side, there in sides:
            fits = jnp.logical_and(there, sec <= k if side else sec < k)

            @pl.when(fits)
            def _():
                hear(sec, side).wait_recv()

    roll = lambda x, by: pltpu.roll(x, by, 1)
    fields = []
    for side, there in sides:
        earlier = jnp.zeros((8, 128), F32)
        for sec in range(secs - 1):
            earlier = earlier + jnp.where(sec < k, e_slots[sec * 3 + 1 + side], 0.0)
        here = e_slots[k * 3 + 1 + side]
        summed = here + jnp.where(lane >= 64, roll(here, 64), 0.0) + (earlier + roll(earlier, 64))
        fields.append(jnp.where(there, summed, 0.0) if side else summed)
    tile_row, tile_col = lane % 64 // 8, lane % 8
    outside = (has_up, True, has_down)
    for sweep in range(SMOOTH):
        new = []
        for n in range(3):
            x = fields[n]
            above = roll(x, 8)
            below = roll(x, 120)
            if n > 0:
                above = jnp.where(tile_row == 0, roll(fields[n - 1], 72), above)
            if n < 2:
                below = jnp.where(tile_row == 7, roll(fields[n + 1], 56), below)
            west = jnp.where(tile_col > 0, roll(x, 1), 0.0)
            east = jnp.where(tile_col < 7, roll(x, 127), 0.0)
            grid_row = (i + n - 1) * 8 + tile_row
            count = (
                (grid_row > 0).astype(F32)
                + (grid_row < areas * 8 - 1).astype(F32)
                + (tile_col > 0).astype(F32)
                + (tile_col < 7).astype(F32)
            )
            above = jnp.where(grid_row > 0, above, 0.0)
            below = jnp.where(grid_row < areas * 8 - 1, below, 0.0)
            mean = (x + (above + below + west + east)) / (1.0 + count)
            new.append(mean if n == 1 else jnp.where(outside[n], mean, 0.0))
        fields = new
    field = fields[1]
    floors = jnp.floor(field)
    field_out[...] = field[0:2]
    whole_out[...] = floors[0:2].astype(jnp.int32)
    frac_out[...] = (field - floors)[0:2]

    for turn in range(chans):
        if turn:
            share(turn).wait_send()

        @pl.when(has_next)
        def _():
            give(turn).wait_send()

    for ahead_by, side, fits in messages:

        @pl.when(fits)
        def _():
            tell(ahead_by, side).wait_send()

    @pl.when(has_down)
    def _():
        near_down.wait_send()

    @pl.when(has_up)
    def _():
        near_up.wait_send()

    @pl.when(has_prev)
    def _():
        coarse_back.wait_send()

    @pl.when(jnp.logical_and(has_next, has_down))
    def _():
        edge_down.wait_send()

    @pl.when(jnp.logical_and(has_next, has_up))
    def _():
        edge_up.wait_send()

    for r in range(1, 4):

        @pl.when(jnp.logical_and(has_down, k >= r))
        def _():
            far_down(r).wait_send()
            far_up(r).wait_recv()

        @pl.when(jnp.logical_and(has_up, k >= r))
        def _():
            far_up(r).wait_send()
            far_down(r).wait_recv()

    keep_top.wait()
    keep_bottom.wait()


def drift_local(devices, coarse, features):
    vm = pl.BlockSpec(memory_space=pltpu.VMEM)
    sm = pl.BlockSpec(memory_space=pltpu.SMEM)
    hbm = pl.BlockSpec(memory_space=pl.ANY)
    dma = pltpu.SemaphoreType.DMA
    small = jax.ShapeDtypeStruct((2, 128), F32)
    halo = jax.ShapeDtypeStruct((2, 16, HALO, 256), BF)
    secs, areas, chans = devices
    return pl.pallas_call(
        functools.partial(drift_kernel, devices),
        out_shape=(small, jax.ShapeDtypeStruct((2, 128), jnp.int32), small, halo, halo),
        in_specs=[sm, vm, hbm],
        out_specs=(vm, vm, vm, hbm, hbm),
        scratch_shapes=[
            pltpu.VMEM((2, 16, 256 + 2 * NEAR, 256), BF),
            pltpu.VMEM((8, 256 + 2 * NEAR, 256), BF),
            pltpu.VMEM((8, 256, 256), BF),
            pltpu.VMEM((2, 128), jnp.int32),
            pltpu.SMEM((2, 128), jnp.int32),
            pltpu.VMEM((2, 128, 2048), BF),
            pltpu.VMEM((2, 192, 2048), BF),
            pltpu.VMEM((3, 128, 192), F32),
            pltpu.VMEM((3, 128, 192), F32),
            pltpu.VMEM((16, 128), F32),
            pltpu.VMEM((16, 128), F32),
            pltpu.VMEM((chans, 16, 128), F32),
            pltpu.VMEM((chans, 16, 128), F32),
            pltpu.VMEM((8, 128), F32),
            pltpu.VMEM((3 * secs, 8, 128), F32),
            dma((2,)), dma((2,)), dma((2,)), dma((2, 4)), dma((2, 4)), dma((2,)), dma((2,)), dma, dma, dma,
            dma((8,)), dma((8,)), dma((8,)), dma((8,)),
            dma((chans,)), dma((chans,)), dma((chans,)), dma((chans,)),
            dma((secs, 3)), dma((3 * secs,)), dma((2,)),
        ],
        compiler_params=pltpu.CompilerParams(
            collective_id=0, has_side_effects=True, vmem_limit_bytes=48 * 2**20
        ),
        name="drift",
    )(coarse, coarse, features)


def warp_kernel(areas, whole, frac, field, feat, top_halo, bottom_halo, out_ref, field_out, held, rows, sems):
    step = pl.program_id(0)
    s = step // 8
    ty = step % 8
    i = lax.axis_index("area")

    def load(part):
        return [
            pltpu.make_async_copy(feat.at[part], held.at[part, :, pl.ds(HALO, 256), :], sems.at[part, 0]),
            pltpu.make_async_copy(top_halo.at[part], held.at[part, :, pl.ds(0, HALO), :], sems.at[part, 1]),
            pltpu.make_async_copy(bottom_halo.at[part], held.at[part, :, pl.ds(HALO + 256, HALO), :], sems.at[part, 2]),
        ]

    def wait(part):
        for copy in load(part):
            copy.wait()

        @pl.when(i == 0)
        def _():
            held[part, :, pl.ds(0, HALO), :] = jnp.zeros((16, HALO, 256), BF)

        @pl.when(i == areas - 1)
        def _():
            held[part, :, pl.ds(HALO + 256, HALO), :] = jnp.zeros((16, HALO, 256), BF)

    @pl.when(step == 0)
    def _():
        for part in range(2):
            for copy in load(part):
                copy.start()
        lane = lax.broadcasted_iota(jnp.int32, (32, 128), 1)
        row = lax.broadcasted_iota(jnp.int32, (32, 128), 0)
        spread = jnp.where(row < 16, field[0:1, :], field[1:2, :])
        spread = jnp.where(lane // 8 == row % 16, spread, 0.0)
        pick = lax.broadcasted_iota(jnp.int32, (128, 8), 0) % 8 == lax.broadcasted_iota(jnp.int32, (128, 8), 1)
        grid = jnp.dot(
            spread, pick.astype(F32), precision=lax.Precision.HIGHEST, preferred_element_type=F32
        )
        field_out[...] = grid.reshape(2, 2, 8, 8)
        wait(0)

    @pl.when(step == 8)
    def _():
        wait(1)

    lane = lax.broadcasted_iota(jnp.int32, (1, 128), 1)
    lane_tile = lane // TILE
    src_col = lax.broadcasted_iota(jnp.int32, (256, 128), 0)
    base = HALO + TILE * ty
    for h in range(2):
        at = step * 8 + 4 * h
        fl_row = [whole[0, at + t] for t in range(4)]
        fl_col = [whole[1, at + t] for t in range(4)]
        fr_row = lane_pick([frac[0, at + t] for t in range(4)], lane_tile)
        fr_col = lane_pick([frac[1, at + t] for t in range(4)], lane_tile)
        low = jnp.minimum(jnp.minimum(fl_row[0], fl_row[1]), jnp.minimum(fl_row[2], fl_row[3]))
        high = jnp.maximum(jnp.maximum(fl_row[0], fl_row[1]), jnp.maximum(fl_row[2], fl_row[3]))
        start = jnp.minimum((base + low) // 16 * 16, 2 * HALO + 256 - 48)
        chunks = (base + high + TILE + 1 - start + 15) // 16
        rel = src_col - (lane + 128 * h + lane_pick(fl_col, lane_tile))
        weight = jnp.where(rel == 0, 1.0 - fr_col, jnp.where(rel == 1, fr_col, 0.0))
        coarse_part = weight.astype(BF)
        fine_part = (weight - coarse_part.astype(F32)).astype(BF)
        mixer = jnp.concatenate([coarse_part, fine_part], 1)

        def chunk(r, _):
            at_row = pl.multiple_of(start + 16 * r, 16)
            block = held[s, :, pl.ds(at_row, 16), :].reshape(256, 256)
            mixed = jnp.dot(block, mixer, preferred_element_type=F32)
            mixed = mixed[:, :128] + mixed[:, 128:]
            rows[:, pl.ds(pl.multiple_of(16 * r, 16), 16), :] = mixed.reshape(16, 16, 128)
            return 0

        for r in range(3):
            chunk(r, 0)
        lax.fori_loop(3, chunks, chunk, 0)
        offs = [base + fl_row[t] - start for t in range(4)]
        for c in range(16):
            upper = rows[c, pl.ds(offs[0], TILE), :]
            lower = rows[c, pl.ds(offs[0] + 1, TILE), :]
            for t in range(1, 4):
                mine = lane_tile == t
                upper = jnp.where(mine, rows[c, pl.ds(offs[t], TILE), :], upper)
                lower = jnp.where(mine, rows[c, pl.ds(offs[t] + 1, TILE), :], lower)
            out_ref[0, c, :, 128 * h : 128 * h + 128] = ((1.0 - fr_row) * upper + fr_row * lower).astype(BF)


def warp_local(areas, whole, frac, field, features, top_halo, bottom_halo):
    sm = pl.BlockSpec(memory_space=pltpu.SMEM)
    hbm = pl.BlockSpec(memory_space=pl.ANY)
    return pl.pallas_call(
        functools.partial(warp_kernel, areas),
        grid=(16,),
        out_shape=(
            jax.ShapeDtypeStruct((2, 16, 256, 256), BF),
            jax.ShapeDtypeStruct((2, 2, 8, 8), F32),
        ),
        in_specs=[sm, sm, pl.BlockSpec(memory_space=pltpu.VMEM), hbm, hbm, hbm],
        out_specs=(
            pl.BlockSpec((1, 16, TILE, 256), lambda g: (g // 8, 0, g % 8, 0)),
            pl.BlockSpec(memory_space=pltpu.VMEM),
        ),
        scratch_shapes=[
            pltpu.VMEM((2, 16, 2 * HALO + 256, 256), BF),
            pltpu.VMEM((16, 176, 128), F32),
            pltpu.SemaphoreType.DMA((2, 3)),
        ],
        compiler_params=pltpu.CompilerParams(vmem_limit_bytes=48 * 2**20),
        name="warp",
    )(whole, frac, field, features, top_halo, bottom_halo)


def local(devices, features, coarse):
    field, whole, frac, top_halo, bottom_halo = drift_local(devices, coarse.reshape(2, 128), features)
    return warp_local(devices[1], whole, frac, field, features, top_halo, bottom_halo)


def solution(mesh):
    placed = (P("sec", "chan", "area", None), P(None, "sec", "area", None))
    devices = tuple(mesh.shape[name] for name in ("sec", "area", "chan"))
    return jax.shard_map(
        functools.partial(local, devices),
        mesh=mesh,
        in_specs=placed,
        out_specs=placed,
        check_vma=False,
    )
```

```python
import functools
import math

import jax
import jax.numpy as jnp
from jax import lax
from jax.experimental import pallas as pl
from jax.experimental.pallas import tpu as pltpu
from jax.sharding import PartitionSpec as P

C = 64
TILE = 32
MAXD = 7
R = 1
SMOOTH = 3
HALO = 64
BF = jnp.bfloat16
F32 = jnp.float32


def lane_pick(scalars, lanes_tile):
    out = jnp.full(lanes_tile.shape, scalars[0])
    for t in range(1, len(scalars)):
        out = jnp.where(lanes_tile == t, scalars[t], out)
    return out


NEAR = 16
WINDOW = 8


def score_rows(f_rows, window, coarse_row, coarse_col, left, right, count):
    src = lax.broadcasted_iota(jnp.int32, (256, 128), 0)
    lane = lax.broadcasted_iota(jnp.int32, (1, 128), 1)
    lane_tile = lane // TILE
    shifts = []
    for h in range(2):
        col = lane + 128 * h + lane_pick([coarse_col[4 * h + t] for t in range(4)], lane_tile)
        rel = src - col
        for b in (-1, 0, 1):
            shifts.append(jnp.where(rel == b, 1.0, 0.0).astype(BF))
    shifted = jnp.concatenate(shifts, 1)
    for c0 in range(0, count, 4):
        moved = lax.dot_general(
            window(c0), shifted, (((1,), (0,)), ((), ())), preferred_element_type=F32
        ).astype(BF)
        for c in range(4):
            for h in range(2):
                for b in range(3):
                    right[h, 64 * b : 64 * b + 64, 128 * (c0 + c) : 128 * (c0 + c) + 128] = moved[
                        64 * c : 64 * c + 64, 384 * h + 128 * b : 384 * h + 128 * b + 128
                    ]
    tile_masks = [lax.broadcasted_iota(jnp.int32, (TILE, 128), 1) // TILE == t for t in range(4)]
    for c in range(count):
        strip = f_rows(c)
        for h in range(2):
            part = strip[:, 128 * h : 128 * h + 128]
            for t in range(4):
                left[h, TILE * t : TILE * t + TILE, 128 * c : 128 * c + 128] = jnp.where(
                    tile_masks[t], part, jnp.zeros_like(part)
                )
    row = lax.broadcasted_iota(jnp.int32, (128, 192), 0)
    col = lax.broadcasted_iota(jnp.int32, (128, 192), 1)
    base = col % 64 - NEAR - row % TILE
    row_tile = lax.broadcasted_iota(jnp.int32, (128, 1), 0) // TILE
    out = [[], [], []]
    for h in range(2):
        gram = lax.dot_general(
            left[h, :, : count * 128],
            right[h, :, : count * 128],
            (((1,), (1,)), ((), ())),
            preferred_element_type=F32,
        )
        rel = base - lane_pick([coarse_row[4 * h + t] for t in range(4)], row_tile)
        for a in range(3):
            kept = jnp.where(rel == a - 1, gram, 0.0)
            out[a].append(jnp.sum(kept.reshape(4, TILE, 192), axis=1))
    return [jnp.concatenate(o, 0) for o in out]


def gather_offsets(acc):
    total = jnp.zeros((16, 128), F32)
    seg = lax.broadcasted_iota(jnp.int32, (16, 192), 1) // 64
    row = lax.broadcasted_iota(jnp.int32, (16, 192), 0)
    for a in range(3):
        pick = (row == seg + 3 * a).astype(F32)
        total = total + lax.dot_general(
            pick, acc[a], (((1,), (1,)), ((), ())), precision=lax.Precision.HIGHEST, preferred_element_type=F32
        )
    return total


def drift_kernel(
    devices, cs, cv, feat,
    field_out, whole_out, frac_out, top_out, bottom_out,
    own, prior, later, later_coarse, later_cs, left, right, acc, acc_later,
    q_send, b_send, q_slots, b_slots, e_send, e_slots,
    load_sem, near_s, near_r, far_s, far_r, edge_s, edge_r, cc_s, cc_r, cc_l,
    a_s, a_r, b_s, b_r, d_s, d_r, g_s, g_r, e_s, e_r, keep_sem,
):
    secs, areas, chans = devices
    k, i, j = (lax.axis_index(name) for name in ("sec", "area", "chan"))
    MESH = pl.DeviceIdType.MESH

    def at(sec, area, chan):
        return {"sec": sec, "area": area, "chan": chan}

    def remote(src, dst, send, recv, target):
        return pltpu.make_async_remote_copy(
            src_ref=src, dst_ref=dst, send_sem=send, recv_sem=recv, device_id=target, device_id_type=MESH
        )

    nxt, prv = lax.rem(k + 1, secs), lax.rem(k + secs - 1, secs)
    down, up = lax.rem(i + 1, areas), lax.rem(i + areas - 1, areas)
    has_next, has_prev = k < secs - 1, k > 0
    has_down, has_up = i < areas - 1, i > 0

    loads = [
        pltpu.make_async_copy(feat.at[s], own.at[s, :, pl.ds(NEAR, 256), :], load_sem.at[s]) for s in range(2)
    ]
    for load in loads:
        load.start()

    barrier = pltpu.get_barrier_semaphore()
    for other in range(secs):
        for side, there in ((-1, has_up), (0, True), (1, has_down)):
            fits = jnp.logical_and(there, jnp.logical_or(side != 0, k != other))

            @pl.when(fits)
            def _():
                pl.semaphore_signal(barrier, inc=1, device_id=at(other, i + side, j), device_id_type=MESH)

    for step, there in ((-1, has_prev), (0, True), (1, has_next)):
        for turn in range(1, chans):

            @pl.when(there)
            def _():
                pl.semaphore_signal(
                    barrier, inc=1, device_id=at(k + step, i, lax.rem(j + turn, chans)), device_id_type=MESH
                )

    one = lambda flag: jnp.where(flag, 1, 0)
    pl.semaphore_wait(
        barrier,
        secs * (1 + one(has_up) + one(has_down)) - 1 + (chans - 1) * (1 + one(has_prev) + one(has_next)),
    )

    heads, tails = pl.ds(0, NEAR), pl.ds(256 - NEAR, NEAR)
    above, below = pl.ds(0, NEAR), pl.ds(NEAR + 256, NEAR)
    near_chans = (pl.ds(0, 16), pl.ds(8, 8))

    def near_down(s):
        return remote(
            feat.at[s, near_chans[s], tails, :], own.at[s, near_chans[s], above, :], near_s.at[0, s], near_r.at[0, s], at(k, down, j)
        )

    def near_up(s):
        return remote(
            feat.at[s, near_chans[s], heads, :], own.at[s, near_chans[s], below, :], near_s.at[1, s], near_r.at[1, s], at(k, up, j)
        )

    relay_up = remote(
        prior.at[:, pl.ds(NEAR, NEAR), :], prior.at[:, below, :], edge_s.at[1], edge_r.at[1], at(k, up, j)
    )
    relay_down = remote(
        prior.at[:, pl.ds(256, NEAR), :], prior.at[:, above, :], edge_s.at[0], edge_r.at[0], at(k, down, j)
    )
    coarse_back = remote(cv, later_coarse, cc_s, cc_r, at(prv, i, j))

    far_parts = [(1, 0, 8, 0), (0, 1, 16, 2), (1, 1, 16, 1), (0, 2, 16, 3), (1, 2, 16, 2), (1, 3, 16, 3)]

    def far_down(n):
        s, r, channels, _ = far_parts[n]
        return remote(
            feat.at[s, pl.ds(0, channels), pl.ds(240 - 16 * r, 16), :],
            top_out.at[s, pl.ds(0, channels), pl.ds(HALO - 16 * (r + 1), 16), :],
            far_s.at[0, n], far_r.at[0, n], at(k, down, j),
        )

    def far_up(n):
        s, r, channels, _ = far_parts[n]
        return remote(
            feat.at[s, pl.ds(0, channels), pl.ds(16 * r, 16), :],
            bottom_out.at[s, pl.ds(0, channels), pl.ds(16 * r, 16), :],
            far_s.at[1, n], far_r.at[1, n], at(k, up, j),
        )

    def ahead(c):
        return remote(
            feat.at[1, pl.ds(0, 8), pl.ds(pl.multiple_of(TILE * c, TILE), TILE), :],
            prior.at[:, pl.ds(pl.multiple_of(NEAR + TILE * c, NEAR), TILE), :],
            a_s.at[c], a_r.at[c], at(nxt, i, j),
        )

    def behind(c):
        return remote(
            feat.at[0, pl.ds(8, 8), pl.ds(pl.multiple_of(TILE * c, TILE), TILE), :],
            later.at[:, pl.ds(pl.multiple_of(TILE * c, TILE), TILE), :],
            b_s.at[c], b_r.at[c], at(prv, i, j),
        )

    def start_parts(c):
        @pl.when(has_next)
        def _():
            ahead(c).start()

        @pl.when(has_prev)
        def _():
            behind(c).start()

    def start_far():
        for n, (_, _, _, first) in enumerate(far_parts):

            @pl.when(jnp.logical_and(has_down, k >= first))
            def _():
                far_down(n).start()

            @pl.when(jnp.logical_and(has_up, k >= first))
            def _():
                far_up(n).start()

    def part_of(n):
        return jnp.where(n == 0, 0, jnp.where(n == 1, 7, n - 1))

    for s in range(2):

        @pl.when(has_down)
        def _():
            near_down(s).start()

        @pl.when(has_up)
        def _():
            near_up(s).start()

    @pl.when(has_prev)
    def _():
        coarse_back.start()

    for n in range(WINDOW):
        start_parts(part_of(n))

    @pl.when(jnp.logical_not(has_next))
    def _():
        start_far()

    @pl.when(jnp.logical_not(has_up))
    def _():
        own[:, :, pl.ds(0, NEAR), :] = jnp.zeros((2, 16, NEAR, 256), BF)
        prior[:, pl.ds(0, NEAR), :] = jnp.zeros((8, NEAR, 256), BF)

    @pl.when(jnp.logical_not(has_down))
    def _():
        own[:, :, pl.ds(NEAR + 256, NEAR), :] = jnp.zeros((2, 16, NEAR, 256), BF)
        prior[:, pl.ds(NEAR + 256, NEAR), :] = jnp.zeros((8, NEAR, 256), BF)

    acc[...] = jnp.zeros_like(acc)
    acc_later[...] = jnp.zeros_like(acc_later)
    for load in loads:
        load.wait()

    keeps = [
        pltpu.make_async_copy(
            own.at[s, near_chans[s], rows, :], halo.at[s, near_chans[s], pl.ds(first, NEAR), :], keep_sem.at[s, side]
        )
        for s in range(2)
        for side, (rows, halo, first) in enumerate(((above, top_out, HALO - NEAR), (below, bottom_out, 0)))
    ]
    for s in range(2):

        @pl.when(has_up)
        def _():
            near_down(s).wait_recv()

        @pl.when(has_down)
        def _():
            near_up(s).wait_recv()

    for keep in keeps:
        keep.start()

    def local_row(ty, _):
        top = pl.multiple_of(ty * TILE, TILE)
        blocks = score_rows(
            lambda c: own[1, c, pl.ds(pl.multiple_of(top + NEAR, NEAR), TILE), :],
            lambda c: own[0, c : c + 4, pl.ds(top, 64), :].reshape(256, 256),
            [cs[0, 64 + ty * 8 + t] for t in range(8)],
            [cs[1, 64 + ty * 8 + t] for t in range(8)],
            left, right, 16,
        )
        for a in range(3):
            acc[a, pl.ds(pl.multiple_of(64 + ty * 8, 8), 8), :] = blocks[a]
        return 0

    lax.fori_loop(0, 8, local_row, 0)

    coarse_local = pltpu.make_async_copy(later_coarse, later_cs, cc_l)

    @pl.when(has_next)
    def _():
        coarse_back.wait_recv()
        coarse_local.start()
        coarse_local.wait()

    def give(turn):
        return remote(b_send, b_slots.at[j], g_s.at[turn], g_r.at[turn], at(nxt, i, lax.rem(j + turn, chans)))

    def prior_row(q, _):
        ty = jnp.where(q < 3, q + 1, jnp.where(q == 3, 0, q))
        top = pl.multiple_of(ty * TILE, TILE)
        blocks = score_rows(
            lambda c: own[0, c, pl.ds(pl.multiple_of(top + NEAR, NEAR), TILE), :],
            lambda c: prior[c : c + 4, pl.ds(top, 64), :].reshape(256, 256),
            [cs[0, ty * 8 + t] for t in range(8)],
            [cs[1, ty * 8 + t] for t in range(8)],
            left, right, 8,
        )
        for a in range(3):
            acc[a, pl.ds(pl.multiple_of(ty * 8, 8), 8), :] = blocks[a]
        return 0

    def remote_row(n, _):
        @pl.when(jnp.logical_and(n == 8, has_next))
        def _():
            b_send[...] = gather_offsets(acc_later)
            for turn in range(chans):
                give(turn).start()

        @pl.when(jnp.logical_and(has_prev, jnp.logical_and(n == 7, has_up)))
        def _():
            relay_down.wait_recv()

        @pl.when(jnp.logical_and(has_prev, jnp.logical_and(n == 8, has_down)))
        def _():
            relay_up.wait_recv()

        @pl.when(has_prev)
        def _():
            first = jnp.where(n < 8, jnp.maximum(n - 4, 0), 5)
            last = jnp.where(n < 4, 0, jnp.where(n < 7, n - 3, jnp.where(n == 7, 5, 8)))
            lax.fori_loop(first, last, prior_row, 0)

        ty = part_of(n)

        @pl.when(jnp.logical_and(has_prev, n < 8))
        def _():
            ahead(ty).wait_recv()
            behind(ty).wait_send()

        @pl.when(jnp.logical_and(has_prev, jnp.logical_and(n == 0, has_up)))
        def _():
            relay_up.start()

        @pl.when(jnp.logical_and(has_prev, jnp.logical_and(n == 1, has_down)))
        def _():
            relay_down.start()

        @pl.when(jnp.logical_and(has_next, n < 8))
        def _():
            behind(ty).wait_recv()
            ahead(ty).wait_send()

        @pl.when(n + WINDOW < 8)
        def _():
            start_parts(part_of(n + WINDOW))

        @pl.when(jnp.logical_and(has_next, n < 8))
        def _():
            top = pl.multiple_of(ty * TILE, TILE)
            blocks = score_rows(
                lambda c: later[c, pl.ds(top, TILE), :],
                lambda c: own[1, 8 + c : 12 + c, pl.ds(top, 64), :].reshape(256, 256),
                [later_cs[0, ty * 8 + t] for t in range(8)],
                [later_cs[1, ty * 8 + t] for t in range(8)],
                left, right, 8,
            )
            for a in range(3):
                acc_later[a, pl.ds(pl.multiple_of(ty * 8, 8), 8), :] = blocks[a]

        return 0

    lax.fori_loop(0, 9, remote_row, 0)

    mine = gather_offsets(acc)
    q_send[...] = mine
    q_slots[j] = mine

    def share(turn):
        return remote(q_send, q_slots.at[j], d_s.at[turn], d_r.at[turn], at(k, i, lax.rem(j + turn, chans)))

    for turn in range(1, chans):
        share(turn).start()

    @pl.when(has_next)
    def _():
        start_far()

    for turn in range(chans):
        if turn:
            share(turn).wait_recv()

        @pl.when(has_prev)
        def _():
            give(turn).wait_recv()

    total = jnp.zeros((16, 128), F32)
    for chan in range(chans):
        total = total + q_slots[chan]
    for chan in range(chans):
        total = total + jnp.where(has_prev, b_slots[chan], 0.0)
    scores = total * (1.0 / math.sqrt(C * TILE * TILE))
    row = lax.broadcasted_iota(jnp.int32, (16, 128), 0)
    weights = jnp.where(row < 9, 1.0 / (1.0 + jnp.exp(-scores)), 0.0)
    weight_total = jnp.sum(weights, axis=0, keepdims=True)
    fine_row = jnp.sum(weights * (row // 3 - 1).astype(F32), axis=0, keepdims=True) / weight_total
    fine_col = jnp.sum(weights * (row % 3 - 1).astype(F32), axis=0, keepdims=True) / weight_total
    lane = lax.broadcasted_iota(jnp.int32, (8, 128), 1)
    comp = lax.broadcasted_iota(jnp.int32, (8, 128), 0)
    moved = cv[...].astype(F32)
    pair = jnp.where(comp == 0, moved[0:1] + fine_row, moved[1:2] + fine_col)
    pair = jnp.where(jnp.logical_and(comp < 2, jnp.logical_or(has_prev, lane >= 64)), pair, 0.0)
    e_send[...] = pair
    e_slots[k * 3 + 1] = pair

    def tell(ahead_by, side):
        slot = k * 3 + 1 - side
        return remote(
            e_send, e_slots.at[slot], e_s.at[ahead_by, side + 1], e_r.at[slot],
            at(lax.rem(k + ahead_by, secs), lax.rem(i + side + areas, areas), j),
        )

    sides = ((-1, has_up), (0, True), (1, has_down))
    messages = [
        (ahead_by, side, jnp.logical_and(there, k + ahead_by < secs))
        for ahead_by in range(secs)
        for side, there in sides
        if ahead_by or side
    ]
    for ahead_by, side, fits in messages:

        @pl.when(fits)
        def _():
            tell(ahead_by, side).start()

    def hear(sec, side):
        return remote(
            e_send, e_slots.at[sec * 3 + 1 + side], e_s.at[0, 0], e_r.at[sec * 3 + 1 + side], at(prv, i, j)
        )

    for sec in range(secs):
        for side, there in sides:
            fits = jnp.logical_and(there, sec <= k if side else sec < k)

            @pl.when(fits)
            def _():
                hear(sec, side).wait_recv()

    roll = lambda x, by: pltpu.roll(x, by, 1)
    fields = []
    for side, there in sides:
        earlier = jnp.zeros((8, 128), F32)
        for sec in range(secs - 1):
            earlier = earlier + jnp.where(sec < k, e_slots[sec * 3 + 1 + side], 0.0)
        here = e_slots[k * 3 + 1 + side]
        summed = here + jnp.where(lane >= 64, roll(here, 64), 0.0) + (earlier + roll(earlier, 64))
        fields.append(jnp.where(there, summed, 0.0) if side else summed)
    tile_row, tile_col = lane % 64 // 8, lane % 8
    outside = (has_up, True, has_down)
    for sweep in range(SMOOTH):
        new = []
        for n in range(3):
            x = fields[n]
            north = roll(x, 8)
            south = roll(x, 120)
            if n > 0:
                north = jnp.where(tile_row == 0, roll(fields[n - 1], 72), north)
            if n < 2:
                south = jnp.where(tile_row == 7, roll(fields[n + 1], 56), south)
            west = jnp.where(tile_col > 0, roll(x, 1), 0.0)
            east = jnp.where(tile_col < 7, roll(x, 127), 0.0)
            grid_row = (i + n - 1) * 8 + tile_row
            count = (
                (grid_row > 0).astype(F32)
                + (grid_row < areas * 8 - 1).astype(F32)
                + (tile_col > 0).astype(F32)
                + (tile_col < 7).astype(F32)
            )
            north = jnp.where(grid_row > 0, north, 0.0)
            south = jnp.where(grid_row < areas * 8 - 1, south, 0.0)
            mean = (x + (north + south + west + east)) / (1.0 + count)
            new.append(mean if n == 1 else jnp.where(outside[n], mean, 0.0))
        fields = new
    field = fields[1]
    floors = jnp.floor(field)
    field_out[...] = field[0:2]
    whole_out[...] = floors[0:2].astype(jnp.int32)
    frac_out[...] = (field - floors)[0:2]

    for turn in range(chans):
        if turn:
            share(turn).wait_send()

        @pl.when(has_next)
        def _():
            give(turn).wait_send()

    for ahead_by, side, fits in messages:

        @pl.when(fits)
        def _():
            tell(ahead_by, side).wait_send()

    for s in range(2):

        @pl.when(has_down)
        def _():
            near_down(s).wait_send()

        @pl.when(has_up)
        def _():
            near_up(s).wait_send()

    @pl.when(has_prev)
    def _():
        coarse_back.wait_send()

    @pl.when(jnp.logical_and(has_prev, has_down))
    def _():
        relay_down.wait_send()

    @pl.when(jnp.logical_and(has_prev, has_up))
    def _():
        relay_up.wait_send()

    for n, (_, _, _, first) in enumerate(far_parts):

        @pl.when(jnp.logical_and(has_down, k >= first))
        def _():
            far_down(n).wait_send()
            far_up(n).wait_recv()

        @pl.when(jnp.logical_and(has_up, k >= first))
        def _():
            far_up(n).wait_send()
            far_down(n).wait_recv()

    for keep in keeps:
        keep.wait()


def drift_local(devices, coarse, features):
    vm = pl.BlockSpec(memory_space=pltpu.VMEM)
    sm = pl.BlockSpec(memory_space=pltpu.SMEM)
    hbm = pl.BlockSpec(memory_space=pl.ANY)
    dma = pltpu.SemaphoreType.DMA
    small = jax.ShapeDtypeStruct((2, 128), F32)
    halo = jax.ShapeDtypeStruct((2, 16, HALO, 256), BF)
    secs, areas, chans = devices
    return pl.pallas_call(
        functools.partial(drift_kernel, devices),
        out_shape=(small, jax.ShapeDtypeStruct((2, 128), jnp.int32), small, halo, halo),
        in_specs=[sm, vm, hbm],
        out_specs=(vm, vm, vm, hbm, hbm),
        scratch_shapes=[
            pltpu.VMEM((2, 16, 256 + 2 * NEAR, 256), BF),
            pltpu.VMEM((8, 256 + 2 * NEAR, 256), BF),
            pltpu.VMEM((8, 256, 256), BF),
            pltpu.VMEM((2, 128), jnp.int32),
            pltpu.SMEM((2, 128), jnp.int32),
            pltpu.VMEM((2, 128, 2048), BF),
            pltpu.VMEM((2, 192, 2048), BF),
            pltpu.VMEM((3, 128, 192), F32),
            pltpu.VMEM((3, 128, 192), F32),
            pltpu.VMEM((16, 128), F32),
            pltpu.VMEM((16, 128), F32),
            pltpu.VMEM((chans, 16, 128), F32),
            pltpu.VMEM((chans, 16, 128), F32),
            pltpu.VMEM((8, 128), F32),
            pltpu.VMEM((3 * secs, 8, 128), F32),
            dma((2,)), dma((2, 2)), dma((2, 2)), dma((2, 6)), dma((2, 6)), dma((2,)), dma((2,)), dma, dma, dma,
            dma((8,)), dma((8,)), dma((8,)), dma((8,)),
            dma((chans,)), dma((chans,)), dma((chans,)), dma((chans,)),
            dma((secs, 3)), dma((3 * secs,)), dma((2, 2)),
        ],
        compiler_params=pltpu.CompilerParams(
            collective_id=0, has_side_effects=True, vmem_limit_bytes=48 * 2**20
        ),
        name="drift",
    )(coarse, coarse, features)


def warp_kernel(
    areas, whole, frac, field, feat, top_halo, bottom_halo, out_ref, field_out, held, rows0, rows1, sems
):
    step = pl.program_id(0)
    s = step // 8
    ty = step % 8
    i = lax.axis_index("area")

    def load(section, part):
        if part == 0:
            halo, there = top_halo, pl.ds(0, HALO)
        else:
            halo, there = bottom_halo, pl.ds(HALO + 256, HALO)
        return [
            pltpu.make_async_copy(
                feat.at[section, :, pl.ds(128 * part, 128), :],
                held.at[section, :, pl.ds(HALO + 128 * part, 128), :],
                sems.at[section, part, 0],
            ),
            pltpu.make_async_copy(halo.at[section], held.at[section, :, there, :], sems.at[section, part, 1]),
        ]

    def start(section, part):
        for copy in load(section, part):
            copy.start()

    def wait(section, part):
        for copy in load(section, part):
            copy.wait()

        @pl.when(i == (0 if part == 0 else areas - 1))
        def _():
            held[section, :, pl.ds(0 if part == 0 else HALO + 256, HALO), :] = jnp.zeros((16, HALO, 256), BF)

    @pl.when(step == 0)
    def _():
        start(0, 0)
        start(0, 1)
        lane = lax.broadcasted_iota(jnp.int32, (32, 128), 1)
        row = lax.broadcasted_iota(jnp.int32, (32, 128), 0)
        spread = jnp.where(row < 16, field[0:1, :], field[1:2, :])
        spread = jnp.where(lane // 8 == row % 16, spread, 0.0)
        pick = lax.broadcasted_iota(jnp.int32, (128, 8), 0) % 8 == lax.broadcasted_iota(jnp.int32, (128, 8), 1)
        grid = jnp.dot(
            spread, pick.astype(F32), precision=lax.Precision.HIGHEST, preferred_element_type=F32
        )
        field_out[...] = grid.reshape(2, 2, 8, 8)
        wait(0, 0)

    @pl.when(step == 2)
    def _():
        start(1, 0)
        start(1, 1)
        wait(0, 1)

    @pl.when(step == 8)
    def _():
        wait(1, 0)
        wait(1, 1)

    lane = lax.broadcasted_iota(jnp.int32, (1, 128), 1)
    lane_tile = lane // TILE
    src_col = lax.broadcasted_iota(jnp.int32, (256, 128), 0)
    base = HALO + TILE * ty
    loaded = jnp.where(step < 2, HALO + 128, 2 * HALO + 256)
    halves = []
    for h in range(2):
        at = step * 8 + 4 * h
        fl_row = [whole[0, at + t] for t in range(4)]
        low = jnp.minimum(jnp.minimum(fl_row[0], fl_row[1]), jnp.minimum(fl_row[2], fl_row[3]))
        high = jnp.maximum(jnp.maximum(fl_row[0], fl_row[1]), jnp.maximum(fl_row[2], fl_row[3]))
        full = (base + low) // 16 * 16
        need = (base + high + TILE + 1 - full + 15) // 16
        halves.append((fl_row, full, need))
    need = jnp.maximum(halves[0][2], halves[1][2])

    def run(n):
        for h in range(2):
            at = step * 8 + 4 * h
            fl_row, full, _ = halves[h]
            rows = (rows0, rows1)[h]
            fl_col = [whole[1, at + t] for t in range(4)]
            fr_row = lane_pick([frac[0, at + t] for t in range(4)], lane_tile)
            fr_col = lane_pick([frac[1, at + t] for t in range(4)], lane_tile)
            rel = src_col - (lane + 128 * h + lane_pick(fl_col, lane_tile))
            weight = jnp.where(rel == 0, 1.0 - fr_col, jnp.where(rel == 1, fr_col, 0.0))
            coarse_part = weight.astype(BF)
            fine_part = (weight - coarse_part.astype(F32)).astype(BF)
            mixer = jnp.concatenate([coarse_part, fine_part], 1)
            start = pl.multiple_of(jnp.minimum(full, loaded - 16 * n), 16)
            block = held[s, :, pl.ds(start, 16 * n), :].reshape(256 * n, 256)
            mixed = jnp.dot(block, mixer, preferred_element_type=F32)
            mixed = mixed[:, :128] + mixed[:, 128:]
            rows[:, 0 : 16 * n, :] = mixed.reshape(16, 16 * n, 128)
            between = [jnp.logical_and(lane_tile == t, fr_row > 0.0) for t in range(4)]
            offs = [base + fl_row[t] - start for t in range(4)]
            for c in range(16):
                upper = rows[c, pl.ds(offs[0], TILE), :]
                lower = jnp.where(between[0], rows[c, pl.ds(offs[0] + 1, TILE), :], 0.0)
                for t in range(1, 4):
                    upper = jnp.where(lane_tile == t, rows[c, pl.ds(offs[t], TILE), :], upper)
                    lower = jnp.where(between[t], rows[c, pl.ds(offs[t] + 1, TILE), :], lower)
                out_ref[0, c, :, 128 * h : 128 * h + 128] = ((1.0 - fr_row) * upper + fr_row * lower).astype(BF)

    least = 0
    for n in (4, 6, 8, 10):
        pl.when(jnp.logical_and(need > least, need <= n))(functools.partial(run, n))
        least = n


def warp_local(areas, whole, frac, field, features, top_halo, bottom_halo):
    sm = pl.BlockSpec(memory_space=pltpu.SMEM)
    hbm = pl.BlockSpec(memory_space=pl.ANY)
    return pl.pallas_call(
        functools.partial(warp_kernel, areas),
        grid=(16,),
        out_shape=(
            jax.ShapeDtypeStruct((2, 16, 256, 256), BF),
            jax.ShapeDtypeStruct((2, 2, 8, 8), F32),
        ),
        in_specs=[sm, sm, pl.BlockSpec(memory_space=pltpu.VMEM), hbm, hbm, hbm],
        out_specs=(
            pl.BlockSpec((1, 16, TILE, 256), lambda g: (g // 8, 0, g % 8, 0)),
            pl.BlockSpec(memory_space=pltpu.VMEM),
        ),
        scratch_shapes=[
            pltpu.VMEM((2, 16, 2 * HALO + 256, 256), BF),
            pltpu.VMEM((16, 160, 128), F32),
            pltpu.VMEM((16, 160, 128), F32),
            pltpu.SemaphoreType.DMA((2, 2, 2)),
        ],
        compiler_params=pltpu.CompilerParams(vmem_limit_bytes=48 * 2**20),
        name="warp",
    )(whole, frac, field, features, top_halo, bottom_halo)


def local(devices, features, coarse):
    field, whole, frac, top_halo, bottom_halo = drift_local(devices, coarse.reshape(2, 128), features)
    return warp_local(devices[1], whole, frac, field, features, top_halo, bottom_halo)


def solution(mesh):
    placed = (P("sec", "chan", "area", None), P(None, "sec", "area", None))
    devices = tuple(mesh.shape[name] for name in ("sec", "area", "chan"))
    return jax.shard_map(
        functools.partial(local, devices),
        mesh=mesh,
        in_specs=placed,
        out_specs=placed,
        check_vma=False,
    )
```

```python
import functools
import math

import jax
import jax.numpy as jnp
from jax import lax
from jax.experimental import pallas as pl
from jax.experimental.pallas import tpu as pltpu
from jax.sharding import PartitionSpec as P

C = 64
TILE = 32
MAXD = 7
R = 1
SMOOTH = 3
HALO = 64
BF = jnp.bfloat16
F32 = jnp.float32


def lane_pick(scalars, lanes_tile):
    out = jnp.full(lanes_tile.shape, scalars[0])
    for t in range(1, len(scalars)):
        out = jnp.where(lanes_tile == t, scalars[t], out)
    return out


NEAR = 16
WINDOW = 5


def score_rows(f_rows, window, coarse_row, coarse_col, left, right, count):
    src = lax.broadcasted_iota(jnp.int32, (256, 128), 0)
    lane = lax.broadcasted_iota(jnp.int32, (1, 128), 1)
    lane_tile = lane // TILE
    shifts = []
    for h in range(2):
        col = lane + 128 * h + lane_pick([coarse_col[4 * h + t] for t in range(4)], lane_tile)
        rel = src - col
        for b in (-1, 0, 1):
            shifts.append(jnp.where(rel == b, 1.0, 0.0).astype(BF))
    shifted = jnp.concatenate(shifts, 1)
    for c0 in range(0, count, 4):
        moved = lax.dot_general(
            window(c0), shifted, (((1,), (0,)), ((), ())), preferred_element_type=F32
        ).astype(BF)
        for c in range(4):
            for h in range(2):
                for b in range(3):
                    right[h, 64 * b : 64 * b + 64, 128 * (c0 + c) : 128 * (c0 + c) + 128] = moved[
                        64 * c : 64 * c + 64, 384 * h + 128 * b : 384 * h + 128 * b + 128
                    ]
    tile_masks = [lax.broadcasted_iota(jnp.int32, (TILE, 128), 1) // TILE == t for t in range(4)]
    for c in range(count):
        strip = f_rows(c)
        for h in range(2):
            part = strip[:, 128 * h : 128 * h + 128]
            for t in range(4):
                left[h, TILE * t : TILE * t + TILE, 128 * c : 128 * c + 128] = jnp.where(
                    tile_masks[t], part, jnp.zeros_like(part)
                )
    row = lax.broadcasted_iota(jnp.int32, (128, 192), 0)
    col = lax.broadcasted_iota(jnp.int32, (128, 192), 1)
    base = col % 64 - NEAR - row % TILE
    row_tile = lax.broadcasted_iota(jnp.int32, (128, 1), 0) // TILE
    out = [[], [], []]
    for h in range(2):
        gram = lax.dot_general(
            left[h, :, : count * 128],
            right[h, :, : count * 128],
            (((1,), (1,)), ((), ())),
            preferred_element_type=F32,
        )
        rel = base - lane_pick([coarse_row[4 * h + t] for t in range(4)], row_tile)
        for a in range(3):
            kept = jnp.where(rel == a - 1, gram, 0.0)
            out[a].append(jnp.sum(kept.reshape(4, TILE, 192), axis=1))
    return [jnp.concatenate(o, 0) for o in out]


def gather_offsets(acc):
    total = jnp.zeros((16, 128), F32)
    seg = lax.broadcasted_iota(jnp.int32, (16, 192), 1) // 64
    row = lax.broadcasted_iota(jnp.int32, (16, 192), 0)
    for a in range(3):
        pick = (row == seg + 3 * a).astype(F32)
        total = total + lax.dot_general(
            pick, acc[a], (((1,), (1,)), ((), ())), precision=lax.Precision.HIGHEST, preferred_element_type=F32
        )
    return total


def drift_kernel(
    devices, cs, cv4, feat,
    field_out, whole_out, frac_out, top_out, bottom_out,
    own, prior, later, cv, later_coarse, later_cs, left, right, lefts, rights, acc, acc_later,
    q_send, b_send, q_slots, b_slots, e_send, e_slots,
    load_sem, near_s, near_r, far_s, far_r, edge_s, edge_r, cc_s, cc_r, cc_l,
    a_s, a_r, b_s, b_r, d_s, d_r, g_s, g_r, e_s, e_r, keep_sem,
):
    secs, areas, chans = devices
    k, i, j = (lax.axis_index(name) for name in ("sec", "area", "chan"))
    MESH = pl.DeviceIdType.MESH

    def at(sec, area, chan):
        return {"sec": sec, "area": area, "chan": chan}

    def remote(src, dst, send, recv, target):
        return pltpu.make_async_remote_copy(
            src_ref=src, dst_ref=dst, send_sem=send, recv_sem=recv, device_id=target, device_id_type=MESH
        )

    nxt, prv = lax.rem(k + 1, secs), lax.rem(k + secs - 1, secs)
    down, up = lax.rem(i + 1, areas), lax.rem(i + areas - 1, areas)
    has_next, has_prev = k < secs - 1, k > 0
    has_down, has_up = i < areas - 1, i > 0

    loads = [
        pltpu.make_async_copy(feat.at[s], own.at[s, :, pl.ds(NEAR, 256), :], load_sem.at[s]) for s in range(2)
    ]
    for load in loads:
        load.start()

    grid_row = lax.broadcasted_iota(jnp.int32, (32, 128), 0) % 16
    grid_lane = lax.broadcasted_iota(jnp.int32, (32, 128), 1)
    column = lax.broadcasted_iota(jnp.int32, (8, 128), 1) % 8 == lax.broadcasted_iota(jnp.int32, (8, 128), 0)
    spread = jnp.dot(
        cv4[...].reshape(32, 8).astype(F32), column.astype(F32), precision=lax.Precision.HIGHEST, preferred_element_type=F32
    )
    spread = jnp.where(grid_lane // 8 == grid_row, spread, 0.0)
    cv[...] = jnp.sum(spread.reshape(2, 16, 128), axis=1).astype(jnp.int32)

    barrier = pltpu.get_barrier_semaphore()
    for other in range(secs):
        for side, there in ((-1, has_up), (0, True), (1, has_down)):
            fits = jnp.logical_and(there, jnp.logical_or(side != 0, k != other))

            @pl.when(fits)
            def _():
                pl.semaphore_signal(barrier, inc=1, device_id=at(other, i + side, j), device_id_type=MESH)

    for step, there in ((-1, has_prev), (0, True), (1, has_next)):
        for turn in range(1, chans):

            @pl.when(there)
            def _():
                pl.semaphore_signal(
                    barrier, inc=1, device_id=at(k + step, i, lax.rem(j + turn, chans)), device_id_type=MESH
                )

    one = lambda flag: jnp.where(flag, 1, 0)
    pl.semaphore_wait(
        barrier,
        secs * (1 + one(has_up) + one(has_down)) - 1 + (chans - 1) * (1 + one(has_prev) + one(has_next)),
    )

    heads, tails = pl.ds(0, NEAR), pl.ds(256 - NEAR, NEAR)
    above, below = pl.ds(0, NEAR), pl.ds(NEAR + 256, NEAR)
    near_chans = (pl.ds(0, 16), pl.ds(8, 8))

    def near_down(s):
        return remote(
            feat.at[s, near_chans[s], tails, :], own.at[s, near_chans[s], above, :], near_s.at[0, s], near_r.at[0, s], at(k, down, j)
        )

    def near_up(s):
        return remote(
            feat.at[s, near_chans[s], heads, :], own.at[s, near_chans[s], below, :], near_s.at[1, s], near_r.at[1, s], at(k, up, j)
        )

    relay_up = remote(
        prior.at[:, pl.ds(NEAR, NEAR), :], prior.at[:, below, :], edge_s.at[1], edge_r.at[1], at(k, up, j)
    )
    relay_down = remote(
        prior.at[:, pl.ds(256, NEAR), :], prior.at[:, above, :], edge_s.at[0], edge_r.at[0], at(k, down, j)
    )
    coarse_back = remote(cv, later_coarse, cc_s, cc_r, at(prv, i, j))

    far_parts = [(1, 0, 8, 0), (0, 1, 16, 2), (1, 1, 16, 1), (0, 2, 16, 3), (1, 2, 16, 2), (1, 3, 16, 3)]

    def far_down(n):
        s, r, channels, _ = far_parts[n]
        return remote(
            feat.at[s, pl.ds(0, channels), pl.ds(240 - 16 * r, 16), :],
            top_out.at[s, pl.ds(0, channels), pl.ds(HALO - 16 * (r + 1), 16), :],
            far_s.at[0, n], far_r.at[0, n], at(k, down, j),
        )

    def far_up(n):
        s, r, channels, _ = far_parts[n]
        return remote(
            feat.at[s, pl.ds(0, channels), pl.ds(16 * r, 16), :],
            bottom_out.at[s, pl.ds(0, channels), pl.ds(16 * r, 16), :],
            far_s.at[1, n], far_r.at[1, n], at(k, up, j),
        )

    def ahead(c):
        return remote(
            feat.at[1, pl.ds(0, 8), pl.ds(pl.multiple_of(TILE * c, TILE), TILE), :],
            prior.at[:, pl.ds(pl.multiple_of(NEAR + TILE * c, NEAR), TILE), :],
            a_s.at[c], a_r.at[c], at(nxt, i, j),
        )

    def behind(c):
        return remote(
            feat.at[0, pl.ds(8, 8), pl.ds(pl.multiple_of(TILE * c, TILE), TILE), :],
            later.at[:, pl.ds(pl.multiple_of(TILE * c, TILE), TILE), :],
            b_s.at[c], b_r.at[c], at(prv, i, j),
        )

    def start_parts(c):
        @pl.when(has_next)
        def _():
            ahead(c).start()

        @pl.when(has_prev)
        def _():
            behind(c).start()

    even = lax.rem(i, 2) == 0

    def start_far(inside, chosen=range(6)):
        goes_down = jnp.logical_and(has_down, even if inside else jnp.logical_not(even))
        goes_up = jnp.logical_and(has_up, jnp.logical_not(even) if inside else even)
        for n in chosen:
            first = far_parts[n][3]

            @pl.when(jnp.logical_and(goes_down, k >= first))
            def _():
                far_down(n).start()

            @pl.when(jnp.logical_and(goes_up, k >= first))
            def _():
                far_up(n).start()

    def part_of(n):
        return jnp.where(n == 0, 0, jnp.where(n == 1, 7, n - 1))

    for s in range(2):

        @pl.when(has_down)
        def _():
            near_down(s).start()

        @pl.when(has_up)
        def _():
            near_up(s).start()

    @pl.when(has_prev)
    def _():
        coarse_back.start()

    for n in range(WINDOW):
        start_parts(part_of(n))

    start_far(True)

    @pl.when(jnp.logical_not(has_up))
    def _():
        own[:, :, pl.ds(0, NEAR), :] = jnp.zeros((2, 16, NEAR, 256), BF)
        prior[:, pl.ds(0, NEAR), :] = jnp.zeros((8, NEAR, 256), BF)

    @pl.when(jnp.logical_not(has_down))
    def _():
        own[:, :, pl.ds(NEAR + 256, NEAR), :] = jnp.zeros((2, 16, NEAR, 256), BF)
        prior[:, pl.ds(NEAR + 256, NEAR), :] = jnp.zeros((8, NEAR, 256), BF)

    acc[...] = jnp.zeros_like(acc)
    acc_later[...] = jnp.zeros_like(acc_later)
    for load in loads:
        load.wait()

    keeps = [
        pltpu.make_async_copy(
            own.at[s, near_chans[s], rows, :], halo.at[s, near_chans[s], pl.ds(first, NEAR), :], keep_sem.at[s, side]
        )
        for s in range(2)
        for side, (rows, halo, first) in enumerate(((above, top_out, HALO - NEAR), (below, bottom_out, 0)))
    ]
    for s in range(2):

        @pl.when(has_up)
        def _():
            near_down(s).wait_recv()

        @pl.when(has_down)
        def _():
            near_up(s).wait_recv()

    for keep in keeps:
        keep.start()

    def local_row(ty, _):
        top = pl.multiple_of(ty * TILE, TILE)
        blocks = score_rows(
            lambda c: own[1, c, pl.ds(pl.multiple_of(top + NEAR, NEAR), TILE), :],
            lambda c: own[0, c : c + 4, pl.ds(top, 64), :].reshape(256, 256),
            [cs[0, 1, ty, t] for t in range(8)],
            [cs[1, 1, ty, t] for t in range(8)],
            left, right, 16,
        )
        for a in range(3):
            acc[a, pl.ds(pl.multiple_of(64 + ty * 8, 8), 8), :] = blocks[a]
        return 0

    lax.fori_loop(0, 8, local_row, 0)

    coarse_local = pltpu.make_async_copy(later_coarse, later_cs, cc_l)

    @pl.when(has_next)
    def _():
        coarse_back.wait_recv()
        coarse_local.start()
        coarse_local.wait()

    def give(turn):
        return remote(b_send, b_slots.at[j], g_s.at[turn], g_r.at[turn], at(nxt, i, lax.rem(j + turn, chans)))

    def prior_row(q, room=0):
        ty = q if isinstance(q, int) else jnp.where(q < 3, q + 1, jnp.where(q == 3, 0, q))
        top = ty * TILE if isinstance(ty, int) else pl.multiple_of(ty * TILE, TILE)
        blocks = score_rows(
            lambda c: own[0, c, pl.ds(top + NEAR if isinstance(ty, int) else pl.multiple_of(top + NEAR, NEAR), TILE), :],
            lambda c: prior[c : c + 4, pl.ds(top, 64), :].reshape(256, 256),
            [cs[0, 0, ty, t] for t in range(8)],
            [cs[1, 0, ty, t] for t in range(8)],
            lefts.at[room], rights.at[room], 8,
        )
        for a in range(3):
            acc[a, pl.ds(ty * 8 if isinstance(ty, int) else pl.multiple_of(ty * 8, 8), 8), :] = blocks[a]
        return 0

    def remote_row(n, _):
        @pl.when(jnp.logical_and(n == 8, has_next))
        def _():
            b_send[...] = gather_offsets(acc_later)
            for turn in range(chans):
                give(turn).start()

        @pl.when(jnp.logical_and(has_prev, jnp.logical_and(n == 7, has_up)))
        def _():
            relay_down.wait_recv()

        @pl.when(jnp.logical_and(has_prev, jnp.logical_and(n == 8, has_down)))
        def _():
            relay_up.wait_recv()

        @pl.when(jnp.logical_and(has_prev, n < 8))
        def _():
            last = jnp.where(n < 4, 0, jnp.where(n < 7, n - 3, 5))
            lax.fori_loop(jnp.maximum(n - 4, 0), last, lambda q, _: prior_row(q), 0)

        @pl.when(jnp.logical_and(has_prev, n == 8))
        def _():
            for room in range(3):
                prior_row(5 + room, room)

        ty = part_of(n)

        @pl.when(jnp.logical_and(has_prev, n < 8))
        def _():
            ahead(ty).wait_recv()
            behind(ty).wait_send()

        @pl.when(jnp.logical_and(has_prev, jnp.logical_and(n == 0, has_up)))
        def _():
            relay_up.start()

        @pl.when(jnp.logical_and(has_prev, jnp.logical_and(n == 1, has_down)))
        def _():
            relay_down.start()

        @pl.when(jnp.logical_and(has_next, n < 8))
        def _():
            behind(ty).wait_recv()
            ahead(ty).wait_send()

        @pl.when(n + WINDOW < 8)
        def _():
            start_parts(part_of(n + WINDOW))

        @pl.when(jnp.logical_and(jnp.logical_not(has_next), n == 8 - WINDOW))
        def _():
            start_far(False)

        @pl.when(jnp.logical_and(has_next, n < 8))
        def _():
            top = pl.multiple_of(ty * TILE, TILE)
            blocks = score_rows(
                lambda c: later[c, pl.ds(top, TILE), :],
                lambda c: own[1, 8 + c : 12 + c, pl.ds(top, 64), :].reshape(256, 256),
                [later_cs[0, ty * 8 + t] for t in range(8)],
                [later_cs[1, ty * 8 + t] for t in range(8)],
                left, right, 8,
            )
            for a in range(3):
                acc_later[a, pl.ds(pl.multiple_of(ty * 8, 8), 8), :] = blocks[a]

        return 0

    lax.fori_loop(0, 9, remote_row, 0)

    mine = gather_offsets(acc)
    q_send[...] = mine
    q_slots[j] = mine

    def share(turn):
        return remote(q_send, q_slots.at[j], d_s.at[turn], d_r.at[turn], at(k, i, lax.rem(j + turn, chans)))

    for turn in range(1, chans):
        share(turn).start()

    @pl.when(has_next)
    def _():
        start_far(False, (0, 1, 2))

    for turn in range(chans):
        if turn:
            share(turn).wait_recv()

        @pl.when(has_prev)
        def _():
            give(turn).wait_recv()

    total = jnp.zeros((16, 128), F32)
    for chan in range(chans):
        total = total + q_slots[chan]
    for chan in range(chans):
        total = total + jnp.where(has_prev, b_slots[chan], 0.0)
    scores = total * (1.0 / math.sqrt(C * TILE * TILE))
    row = lax.broadcasted_iota(jnp.int32, (16, 128), 0)
    weights = jnp.where(row < 9, 1.0 / (1.0 + jnp.exp(-scores)), 0.0)
    weight_total = jnp.sum(weights, axis=0, keepdims=True)
    fine_row = jnp.sum(weights * (row // 3 - 1).astype(F32), axis=0, keepdims=True) / weight_total
    fine_col = jnp.sum(weights * (row % 3 - 1).astype(F32), axis=0, keepdims=True) / weight_total
    lane = lax.broadcasted_iota(jnp.int32, (8, 128), 1)
    comp = lax.broadcasted_iota(jnp.int32, (8, 128), 0)
    moved = cv[...].astype(F32)
    pair = jnp.where(comp == 0, moved[0:1] + fine_row, moved[1:2] + fine_col)
    pair = jnp.where(jnp.logical_and(comp < 2, jnp.logical_or(has_prev, lane >= 64)), pair, 0.0)
    e_send[...] = pair
    e_slots[k * 3 + 1] = pair

    def tell(ahead_by, side):
        slot = k * 3 + 1 - side
        return remote(
            e_send, e_slots.at[slot], e_s.at[ahead_by, side + 1], e_r.at[slot],
            at(lax.rem(k + ahead_by, secs), lax.rem(i + side + areas, areas), j),
        )

    sides = ((-1, has_up), (0, True), (1, has_down))
    messages = [
        (ahead_by, side, jnp.logical_and(there, k + ahead_by < secs))
        for ahead_by in range(secs)
        for side, there in sides
        if ahead_by or side
    ]
    for ahead_by, side, fits in messages:

        @pl.when(fits)
        def _():
            tell(ahead_by, side).start()

    @pl.when(has_next)
    def _():
        start_far(False, (3, 4, 5))

    def hear(sec, side):
        return remote(
            e_send, e_slots.at[sec * 3 + 1 + side], e_s.at[0, 0], e_r.at[sec * 3 + 1 + side], at(prv, i, j)
        )

    for sec in range(secs):
        for side, there in sides:
            fits = jnp.logical_and(there, sec <= k if side else sec < k)

            @pl.when(fits)
            def _():
                hear(sec, side).wait_recv()

    roll = lambda x, by: pltpu.roll(x, by, 1)
    fields = []
    for side, there in sides:
        earlier = jnp.zeros((8, 128), F32)
        for sec in range(secs - 1):
            earlier = earlier + jnp.where(sec < k, e_slots[sec * 3 + 1 + side], 0.0)
        here = e_slots[k * 3 + 1 + side]
        summed = here + jnp.where(lane >= 64, roll(here, 64), 0.0) + (earlier + roll(earlier, 64))
        fields.append(jnp.where(there, summed, 0.0) if side else summed)
    tile_row, tile_col = lane % 64 // 8, lane % 8
    outside = (has_up, True, has_down)
    for sweep in range(SMOOTH):
        new = []
        for n in range(3):
            x = fields[n]
            north = roll(x, 8)
            south = roll(x, 120)
            if n > 0:
                north = jnp.where(tile_row == 0, roll(fields[n - 1], 72), north)
            if n < 2:
                south = jnp.where(tile_row == 7, roll(fields[n + 1], 56), south)
            west = jnp.where(tile_col > 0, roll(x, 1), 0.0)
            east = jnp.where(tile_col < 7, roll(x, 127), 0.0)
            grid_row = (i + n - 1) * 8 + tile_row
            count = (
                (grid_row > 0).astype(F32)
                + (grid_row < areas * 8 - 1).astype(F32)
                + (tile_col > 0).astype(F32)
                + (tile_col < 7).astype(F32)
            )
            north = jnp.where(grid_row > 0, north, 0.0)
            south = jnp.where(grid_row < areas * 8 - 1, south, 0.0)
            mean = (x + (north + south + west + east)) / (1.0 + count)
            new.append(mean if n == 1 else jnp.where(outside[n], mean, 0.0))
        fields = new
    field = fields[1]
    floors = jnp.floor(field)
    field_out[...] = field[0:2]
    whole_out[...] = floors[0:2].astype(jnp.int32)
    frac_out[...] = (field - floors)[0:2]

    for turn in range(chans):
        if turn:
            share(turn).wait_send()

        @pl.when(has_next)
        def _():
            give(turn).wait_send()

    for ahead_by, side, fits in messages:

        @pl.when(fits)
        def _():
            tell(ahead_by, side).wait_send()

    for s in range(2):

        @pl.when(has_down)
        def _():
            near_down(s).wait_send()

        @pl.when(has_up)
        def _():
            near_up(s).wait_send()

    @pl.when(has_prev)
    def _():
        coarse_back.wait_send()

    @pl.when(jnp.logical_and(has_prev, has_down))
    def _():
        relay_down.wait_send()

    @pl.when(jnp.logical_and(has_prev, has_up))
    def _():
        relay_up.wait_send()

    for n, (_, _, _, first) in enumerate(far_parts):

        @pl.when(jnp.logical_and(has_down, k >= first))
        def _():
            far_down(n).wait_send()
            far_up(n).wait_recv()

        @pl.when(jnp.logical_and(has_up, k >= first))
        def _():
            far_up(n).wait_send()
            far_down(n).wait_recv()

    for keep in keeps:
        keep.wait()


def drift_local(devices, coarse, features):
    vm = pl.BlockSpec(memory_space=pltpu.VMEM)
    sm = pl.BlockSpec(memory_space=pltpu.SMEM)
    hbm = pl.BlockSpec(memory_space=pl.ANY)
    dma = pltpu.SemaphoreType.DMA
    small = jax.ShapeDtypeStruct((2, 128), F32)
    halo = jax.ShapeDtypeStruct((2, 16, HALO, 256), BF)
    secs, areas, chans = devices
    return pl.pallas_call(
        functools.partial(drift_kernel, devices),
        out_shape=(small, jax.ShapeDtypeStruct((2, 128), jnp.int32), small, halo, halo),
        in_specs=[sm, vm, hbm],
        out_specs=(vm, vm, vm, hbm, hbm),
        scratch_shapes=[
            pltpu.VMEM((2, 16, 256 + 2 * NEAR, 256), BF),
            pltpu.VMEM((8, 256 + 2 * NEAR, 256), BF),
            pltpu.VMEM((8, 256, 256), BF),
            pltpu.VMEM((2, 128), jnp.int32),
            pltpu.VMEM((2, 128), jnp.int32),
            pltpu.SMEM((2, 128), jnp.int32),
            pltpu.VMEM((2, 128, 2048), BF),
            pltpu.VMEM((2, 192, 2048), BF),
            pltpu.VMEM((3, 2, 128, 1024), BF),
            pltpu.VMEM((3, 2, 192, 1024), BF),
            pltpu.VMEM((3, 128, 192), F32),
            pltpu.VMEM((3, 128, 192), F32),
            pltpu.VMEM((16, 128), F32),
            pltpu.VMEM((16, 128), F32),
            pltpu.VMEM((chans, 16, 128), F32),
            pltpu.VMEM((chans, 16, 128), F32),
            pltpu.VMEM((8, 128), F32),
            pltpu.VMEM((3 * secs, 8, 128), F32),
            dma((2,)), dma((2, 2)), dma((2, 2)), dma((2, 6)), dma((2, 6)), dma((2,)), dma((2,)), dma, dma, dma,
            dma((8,)), dma((8,)), dma((8,)), dma((8,)),
            dma((chans,)), dma((chans,)), dma((chans,)), dma((chans,)),
            dma((secs, 3)), dma((3 * secs,)), dma((2, 2)),
        ],
        compiler_params=pltpu.CompilerParams(
            collective_id=0, has_side_effects=True, vmem_limit_bytes=48 * 2**20
        ),
        name="drift",
    )(coarse, coarse, features)


def warp_kernel(
    areas, whole, frac, field, feat, top_halo, bottom_halo, out_ref, field_out, held, rows_all, sems
):
    step = pl.program_id(0)
    s = step // 4
    ty0 = step % 4 * 2
    i = lax.axis_index("area")

    def load(section, part):
        if part == 0:
            halo, there = top_halo, pl.ds(0, HALO)
        else:
            halo, there = bottom_halo, pl.ds(HALO + 256, HALO)
        return [
            pltpu.make_async_copy(
                feat.at[section, :, pl.ds(128 * part, 128), :],
                held.at[section, :, pl.ds(HALO + 128 * part, 128), :],
                sems.at[section, part, 0],
            ),
            pltpu.make_async_copy(halo.at[section], held.at[section, :, there, :], sems.at[section, part, 1]),
        ]

    def start(section, part):
        for copy in load(section, part):
            copy.start()

    def wait(section, part):
        for copy in load(section, part):
            copy.wait()

        @pl.when(i == (0 if part == 0 else areas - 1))
        def _():
            held[section, :, pl.ds(0 if part == 0 else HALO + 256, HALO), :] = jnp.zeros((16, HALO, 256), BF)

    @pl.when(step == 0)
    def _():
        start(0, 0)
        start(0, 1)
        lane = lax.broadcasted_iota(jnp.int32, (32, 128), 1)
        row = lax.broadcasted_iota(jnp.int32, (32, 128), 0)
        spread = jnp.where(row < 16, field[0:1, :], field[1:2, :])
        spread = jnp.where(lane // 8 == row % 16, spread, 0.0)
        pick = lax.broadcasted_iota(jnp.int32, (128, 8), 0) % 8 == lax.broadcasted_iota(jnp.int32, (128, 8), 1)
        grid = jnp.dot(
            spread, pick.astype(F32), precision=lax.Precision.HIGHEST, preferred_element_type=F32
        )
        field_out[...] = grid.reshape(2, 2, 8, 8)
        wait(0, 0)

    @pl.when(step == 1)
    def _():
        start(1, 0)
        start(1, 1)
        wait(0, 1)

    @pl.when(step == 4)
    def _():
        wait(1, 0)
        wait(1, 1)

    lane = lax.broadcasted_iota(jnp.int32, (1, 128), 1)
    lane_tile = lane // TILE
    src_col = lax.broadcasted_iota(jnp.int32, (256, 128), 0)
    parts = []
    need = jnp.int32(0)
    for q in range(2):
        base = HALO + TILE * (ty0 + q)
        for h in range(2):
            at = s * 64 + (ty0 + q) * 8 + 4 * h
            fl_row = [whole[0, at + t] for t in range(4)]
            low = jnp.minimum(jnp.minimum(fl_row[0], fl_row[1]), jnp.minimum(fl_row[2], fl_row[3]))
            high = jnp.maximum(jnp.maximum(fl_row[0], fl_row[1]), jnp.maximum(fl_row[2], fl_row[3]))
            full = (base + low) // 16 * 16
            need = jnp.maximum(need, (base + high + TILE + 1 - full + 15) // 16)
            parts.append((q, h, at, base, fl_row, full))
    loaded = jnp.where(jnp.logical_and(s == 0, ty0 < 2), 192, 2 * HALO + 256)

    def run(n):
        for q, h, at, base, fl_row, full in parts:
            rows = rows_all.at[2 * q + h]
            fl_col = [whole[1, at + t] for t in range(4)]
            fr_row = lane_pick([frac[0, at + t] for t in range(4)], lane_tile)
            fr_col = lane_pick([frac[1, at + t] for t in range(4)], lane_tile)
            rel = src_col - (lane + 128 * h + lane_pick(fl_col, lane_tile))
            weight = jnp.where(rel == 0, 1.0 - fr_col, jnp.where(rel == 1, fr_col, 0.0))
            coarse_part = weight.astype(BF)
            fine_part = (weight - coarse_part.astype(F32)).astype(BF)
            mixer = jnp.concatenate([coarse_part, fine_part], 1)
            start = pl.multiple_of(jnp.minimum(full, loaded - 16 * n), 16)
            block = held[s, :, pl.ds(start, 16 * n), :].reshape(256 * n, 256)
            mixed = jnp.dot(block, mixer, preferred_element_type=F32)
            mixed = mixed[:, :128] + mixed[:, 128:]
            rows[:, 0 : 16 * n, :] = mixed.reshape(16, 16 * n, 128)
            between = [jnp.logical_and(lane_tile == t, fr_row > 0.0) for t in range(4)]
            offs = [base + fl_row[t] - start for t in range(4)]
            for c in range(16):
                upper = rows[c, pl.ds(offs[0], TILE), :]
                lower = jnp.where(between[0], rows[c, pl.ds(offs[0] + 1, TILE), :], 0.0)
                for t in range(1, 4):
                    upper = jnp.where(lane_tile == t, rows[c, pl.ds(offs[t], TILE), :], upper)
                    lower = jnp.where(between[t], rows[c, pl.ds(offs[t] + 1, TILE), :], lower)
                out_ref[0, c, TILE * q : TILE * q + TILE, 128 * h : 128 * h + 128] = (
                    (1.0 - fr_row) * upper + fr_row * lower
                ).astype(BF)

    least = 0
    for n in (4, 6, 8, 10):
        pl.when(jnp.logical_and(need > least, need <= n))(functools.partial(run, n))
        least = n


def warp_local(areas, whole, frac, field, features, top_halo, bottom_halo):
    sm = pl.BlockSpec(memory_space=pltpu.SMEM)
    hbm = pl.BlockSpec(memory_space=pl.ANY)
    return pl.pallas_call(
        functools.partial(warp_kernel, areas),
        grid=(8,),
        out_shape=(
            jax.ShapeDtypeStruct((2, 16, 256, 256), BF),
            jax.ShapeDtypeStruct((2, 2, 8, 8), F32),
        ),
        in_specs=[sm, sm, pl.BlockSpec(memory_space=pltpu.VMEM), hbm, hbm, hbm],
        out_specs=(
            pl.BlockSpec((1, 16, 2 * TILE, 256), lambda g: (g // 4, 0, g % 4, 0)),
            pl.BlockSpec(memory_space=pltpu.VMEM),
        ),
        scratch_shapes=[
            pltpu.VMEM((2, 16, 2 * HALO + 256, 256), BF),
            pltpu.VMEM((4, 16, 160, 128), F32),
            pltpu.SemaphoreType.DMA((2, 2, 2)),
        ],
        compiler_params=pltpu.CompilerParams(vmem_limit_bytes=48 * 2**20),
        name="warp",
    )(whole, frac, field, features, top_halo, bottom_halo)


def local(devices, features, coarse):
    field, whole, frac, top_halo, bottom_halo = drift_local(devices, coarse, features)
    return warp_local(devices[1], whole, frac, field, features, top_halo, bottom_halo)


def solution(mesh):
    placed = (P("sec", "chan", "area", None), P(None, "sec", "area", None))
    devices = tuple(mesh.shape[name] for name in ("sec", "area", "chan"))
    return jax.shard_map(
        functools.partial(local, devices),
        mesh=mesh,
        in_specs=placed,
        out_specs=placed,
        check_vma=False,
    )
```

```python
import functools
import math

import jax
import jax.numpy as jnp
from jax import lax
from jax.experimental import pallas as pl
from jax.experimental.pallas import tpu as pltpu
from jax.sharding import PartitionSpec as P

C = 64
TILE = 32
MAXD = 7
R = 1
SMOOTH = 3
HALO = 64
BF = jnp.bfloat16
F32 = jnp.float32


def lane_pick(scalars, lanes_tile):
    out = jnp.full(lanes_tile.shape, scalars[0])
    for t in range(1, len(scalars)):
        out = jnp.where(lanes_tile == t, scalars[t], out)
    return out


NEAR = 16
WINDOW = 5


def score_rows(f_rows, window, coarse_row, coarse_col, left, right, count):
    src = lax.broadcasted_iota(jnp.int32, (256, 128), 0)
    lane = lax.broadcasted_iota(jnp.int32, (1, 128), 1)
    lane_tile = lane // TILE
    shifts = []
    for h in range(2):
        col = lane + 128 * h + lane_pick([coarse_col[4 * h + t] for t in range(4)], lane_tile)
        rel = src - col
        for b in (-1, 0, 1):
            shifts.append(jnp.where(rel == b, 1.0, 0.0).astype(BF))
    shifted = jnp.concatenate(shifts, 1)
    for c0 in range(0, count, 4):
        moved = lax.dot_general(
            window(c0), shifted, (((1,), (0,)), ((), ())), preferred_element_type=F32
        ).astype(BF)
        for c in range(4):
            for h in range(2):
                for b in range(3):
                    right[h, 64 * b : 64 * b + 64, 128 * (c0 + c) : 128 * (c0 + c) + 128] = moved[
                        64 * c : 64 * c + 64, 384 * h + 128 * b : 384 * h + 128 * b + 128
                    ]
    tile_masks = [lax.broadcasted_iota(jnp.int32, (TILE, 128), 1) // TILE == t for t in range(4)]
    for c in range(count):
        strip = f_rows(c)
        for h in range(2):
            part = strip[:, 128 * h : 128 * h + 128]
            for t in range(4):
                left[h, TILE * t : TILE * t + TILE, 128 * c : 128 * c + 128] = jnp.where(
                    tile_masks[t], part, jnp.zeros_like(part)
                )
    row = lax.broadcasted_iota(jnp.int32, (128, 192), 0)
    col = lax.broadcasted_iota(jnp.int32, (128, 192), 1)
    base = col % 64 - NEAR - row % TILE
    row_tile = lax.broadcasted_iota(jnp.int32, (128, 1), 0) // TILE
    out = [[], [], []]
    for h in range(2):
        gram = lax.dot_general(
            left[h, :, : count * 128],
            right[h, :, : count * 128],
            (((1,), (1,)), ((), ())),
            preferred_element_type=F32,
        )
        rel = base - lane_pick([coarse_row[4 * h + t] for t in range(4)], row_tile)
        for a in range(3):
            kept = jnp.where(rel == a - 1, gram, 0.0)
            out[a].append(jnp.sum(kept.reshape(4, TILE, 192), axis=1))
    return [jnp.concatenate(o, 0) for o in out]


def gather_offsets(acc):
    total = jnp.zeros((16, 128), F32)
    seg = lax.broadcasted_iota(jnp.int32, (16, 192), 1) // 64
    row = lax.broadcasted_iota(jnp.int32, (16, 192), 0)
    for a in range(3):
        pick = (row == seg + 3 * a).astype(F32)
        total = total + lax.dot_general(
            pick, acc[a], (((1,), (1,)), ((), ())), precision=lax.Precision.HIGHEST, preferred_element_type=F32
        )
    return total


def drift_kernel(
    devices, cs, cv4, feat,
    field_out, whole_out, frac_out, top_out, bottom_out,
    own, prior, later, cv, later_coarse, later_cs, left, right, lefts, rights, acc, acc_later,
    q_send, b_send, q_slots, b_slots, e_send, e_slots,
    load_sem, near_s, near_r, far_s, far_r, edge_s, edge_r, cc_s, cc_r, cc_l,
    a_s, a_r, b_s, b_r, d_s, d_r, g_s, g_r, e_s, e_r, keep_sem,
):
    secs, areas, chans = devices
    k, i, j = (lax.axis_index(name) for name in ("sec", "area", "chan"))
    MESH = pl.DeviceIdType.MESH

    def at(sec, area, chan):
        return {"sec": sec, "area": area, "chan": chan}

    def remote(src, dst, send, recv, target):
        return pltpu.make_async_remote_copy(
            src_ref=src, dst_ref=dst, send_sem=send, recv_sem=recv, device_id=target, device_id_type=MESH
        )

    nxt, prv = lax.rem(k + 1, secs), lax.rem(k + secs - 1, secs)
    down, up = lax.rem(i + 1, areas), lax.rem(i + areas - 1, areas)
    has_next, has_prev = k < secs - 1, k > 0
    has_down, has_up = i < areas - 1, i > 0

    loads = [
        pltpu.make_async_copy(feat.at[s], own.at[s, :, pl.ds(NEAR, 256), :], load_sem.at[s]) for s in range(2)
    ]
    for load in loads:
        load.start()

    barrier = pltpu.get_barrier_semaphore()
    for other in range(secs):
        for side, there in ((-1, has_up), (0, True), (1, has_down)):
            fits = jnp.logical_and(there, jnp.logical_or(side != 0, k != other))

            @pl.when(fits)
            def _():
                pl.semaphore_signal(barrier, inc=1, device_id=at(other, i + side, j), device_id_type=MESH)

    for step, there in ((-1, has_prev), (0, True), (1, has_next)):
        for turn in range(1, chans):

            @pl.when(there)
            def _():
                pl.semaphore_signal(
                    barrier, inc=1, device_id=at(k + step, i, lax.rem(j + turn, chans)), device_id_type=MESH
                )

    one = lambda flag: jnp.where(flag, 1, 0)
    pl.semaphore_wait(
        barrier,
        secs * (1 + one(has_up) + one(has_down)) - 1 + (chans - 1) * (1 + one(has_prev) + one(has_next)),
    )

    heads, tails = pl.ds(0, NEAR), pl.ds(256 - NEAR, NEAR)
    above, below = pl.ds(0, NEAR), pl.ds(NEAR + 256, NEAR)
    near_chans = (pl.ds(0, 16), pl.ds(8, 8))

    def near_down(s):
        return remote(
            feat.at[s, near_chans[s], tails, :], own.at[s, near_chans[s], above, :], near_s.at[0, s], near_r.at[0, s], at(k, down, j)
        )

    def near_up(s):
        return remote(
            feat.at[s, near_chans[s], heads, :], own.at[s, near_chans[s], below, :], near_s.at[1, s], near_r.at[1, s], at(k, up, j)
        )

    relay_up = remote(
        prior.at[:, pl.ds(NEAR, NEAR), :], prior.at[:, below, :], edge_s.at[1], edge_r.at[1], at(k, up, j)
    )
    relay_down = remote(
        prior.at[:, pl.ds(256, NEAR), :], prior.at[:, above, :], edge_s.at[0], edge_r.at[0], at(k, down, j)
    )
    coarse_back = remote(cv, later_coarse, cc_s, cc_r, at(prv, i, j))

    far_parts = [(1, 0, 8, 0), (0, 1, 16, 2), (1, 1, 16, 1), (0, 2, 16, 3), (1, 2, 16, 2), (1, 3, 16, 3)]

    def far_down(n):
        s, r, channels, _ = far_parts[n]
        return remote(
            feat.at[s, pl.ds(0, channels), pl.ds(240 - 16 * r, 16), :],
            top_out.at[s, pl.ds(0, channels), pl.ds(HALO - 16 * (r + 1), 16), :],
            far_s.at[0, n], far_r.at[0, n], at(k, down, j),
        )

    def far_up(n):
        s, r, channels, _ = far_parts[n]
        return remote(
            feat.at[s, pl.ds(0, channels), pl.ds(16 * r, 16), :],
            bottom_out.at[s, pl.ds(0, channels), pl.ds(16 * r, 16), :],
            far_s.at[1, n], far_r.at[1, n], at(k, up, j),
        )

    def ahead(c):
        return remote(
            feat.at[1, pl.ds(0, 8), pl.ds(pl.multiple_of(TILE * c, TILE), TILE), :],
            prior.at[:, pl.ds(pl.multiple_of(NEAR + TILE * c, NEAR), TILE), :],
            a_s.at[c], a_r.at[c], at(nxt, i, j),
        )

    def behind(c):
        return remote(
            feat.at[0, pl.ds(8, 8), pl.ds(pl.multiple_of(TILE * c, TILE), TILE), :],
            later.at[:, pl.ds(pl.multiple_of(TILE * c, TILE), TILE), :],
            b_s.at[c], b_r.at[c], at(prv, i, j),
        )

    def start_parts(c):
        @pl.when(has_next)
        def _():
            ahead(c).start()

        @pl.when(has_prev)
        def _():
            behind(c).start()

    even = lax.rem(i, 2) == 0

    def start_far(inside, chosen=range(6)):
        goes_down = jnp.logical_and(has_down, even if inside else jnp.logical_not(even))
        goes_up = jnp.logical_and(has_up, jnp.logical_not(even) if inside else even)
        for n in chosen:
            first = far_parts[n][3]

            @pl.when(jnp.logical_and(goes_down, k >= first))
            def _():
                far_down(n).start()

            @pl.when(jnp.logical_and(goes_up, k >= first))
            def _():
                far_up(n).start()

    def part_of(n):
        return jnp.where(n == 0, 0, jnp.where(n == 1, 7, n - 1))

    for s in range(2):

        @pl.when(has_down)
        def _():
            near_down(s).start()

        @pl.when(has_up)
        def _():
            near_up(s).start()

    for n in range(WINDOW):
        start_parts(part_of(n))

    grid_row = lax.broadcasted_iota(jnp.int32, (32, 128), 0) % 16
    grid_lane = lax.broadcasted_iota(jnp.int32, (32, 128), 1)
    column = lax.broadcasted_iota(jnp.int32, (8, 128), 1) % 8 == lax.broadcasted_iota(jnp.int32, (8, 128), 0)
    spread = jnp.dot(
        cv4[...].reshape(32, 8).astype(F32), column.astype(F32), precision=lax.Precision.HIGHEST, preferred_element_type=F32
    )
    spread = jnp.where(grid_lane // 8 == grid_row, spread, 0.0)
    cv[...] = jnp.sum(spread.reshape(2, 16, 128), axis=1).astype(jnp.int32)

    @pl.when(has_prev)
    def _():
        coarse_back.start()

    start_far(True)

    @pl.when(jnp.logical_not(has_up))
    def _():
        own[:, :, pl.ds(0, NEAR), :] = jnp.zeros((2, 16, NEAR, 256), BF)
        prior[:, pl.ds(0, NEAR), :] = jnp.zeros((8, NEAR, 256), BF)

    @pl.when(jnp.logical_not(has_down))
    def _():
        own[:, :, pl.ds(NEAR + 256, NEAR), :] = jnp.zeros((2, 16, NEAR, 256), BF)
        prior[:, pl.ds(NEAR + 256, NEAR), :] = jnp.zeros((8, NEAR, 256), BF)

    acc[...] = jnp.zeros_like(acc)
    acc_later[...] = jnp.zeros_like(acc_later)
    for load in loads:
        load.wait()

    keeps = [
        pltpu.make_async_copy(
            own.at[s, near_chans[s], rows, :], halo.at[s, near_chans[s], pl.ds(first, NEAR), :], keep_sem.at[s, side]
        )
        for s in range(2)
        for side, (rows, halo, first) in enumerate(((above, top_out, HALO - NEAR), (below, bottom_out, 0)))
    ]
    for s in range(2):

        @pl.when(has_up)
        def _():
            near_down(s).wait_recv()

        @pl.when(has_down)
        def _():
            near_up(s).wait_recv()

    for keep in keeps:
        keep.start()

    def local_row(ty, _):
        top = pl.multiple_of(ty * TILE, TILE)
        blocks = score_rows(
            lambda c: own[1, c, pl.ds(pl.multiple_of(top + NEAR, NEAR), TILE), :],
            lambda c: own[0, c : c + 4, pl.ds(top, 64), :].reshape(256, 256),
            [cs[0, 1, ty, t] for t in range(8)],
            [cs[1, 1, ty, t] for t in range(8)],
            left, right, 16,
        )
        for a in range(3):
            acc[a, pl.ds(pl.multiple_of(64 + ty * 8, 8), 8), :] = blocks[a]
        return 0

    lax.fori_loop(0, 8, local_row, 0)

    coarse_local = pltpu.make_async_copy(later_coarse, later_cs, cc_l)

    @pl.when(has_next)
    def _():
        coarse_back.wait_recv()
        coarse_local.start()
        coarse_local.wait()

    def give(turn):
        return remote(b_send, b_slots.at[j], g_s.at[turn], g_r.at[turn], at(nxt, i, lax.rem(j + turn, chans)))

    def prior_row(q, room=0):
        ty = q if isinstance(q, int) else jnp.where(q < 3, q + 1, jnp.where(q == 3, 0, q))
        top = ty * TILE if isinstance(ty, int) else pl.multiple_of(ty * TILE, TILE)
        blocks = score_rows(
            lambda c: own[0, c, pl.ds(top + NEAR if isinstance(ty, int) else pl.multiple_of(top + NEAR, NEAR), TILE), :],
            lambda c: prior[c : c + 4, pl.ds(top, 64), :].reshape(256, 256),
            [cs[0, 0, ty, t] for t in range(8)],
            [cs[1, 0, ty, t] for t in range(8)],
            lefts.at[room], rights.at[room], 8,
        )
        for a in range(3):
            acc[a, pl.ds(ty * 8 if isinstance(ty, int) else pl.multiple_of(ty * 8, 8), 8), :] = blocks[a]
        return 0

    def remote_row(n, _):
        @pl.when(jnp.logical_and(n == 8, has_next))
        def _():
            b_send[...] = gather_offsets(acc_later)
            for turn in range(chans):
                give(turn).start()

        @pl.when(jnp.logical_and(has_prev, jnp.logical_and(n == 7, has_up)))
        def _():
            relay_down.wait_recv()

        @pl.when(jnp.logical_and(has_prev, jnp.logical_and(n == 8, has_down)))
        def _():
            relay_up.wait_recv()

        @pl.when(jnp.logical_and(has_prev, n < 8))
        def _():
            last = jnp.where(n < 4, 0, jnp.where(n < 7, n - 3, 5))
            lax.fori_loop(jnp.maximum(n - 4, 0), last, lambda q, _: prior_row(q), 0)

        @pl.when(jnp.logical_and(has_prev, n == 8))
        def _():
            for room in range(3):
                prior_row(5 + room, room)

        ty = part_of(n)

        @pl.when(jnp.logical_and(has_prev, n < 8))
        def _():
            ahead(ty).wait_recv()
            behind(ty).wait_send()

        @pl.when(jnp.logical_and(has_prev, jnp.logical_and(n == 0, has_up)))
        def _():
            relay_up.start()

        @pl.when(jnp.logical_and(has_prev, jnp.logical_and(n == 1, has_down)))
        def _():
            relay_down.start()

        @pl.when(jnp.logical_and(has_next, n < 8))
        def _():
            behind(ty).wait_recv()
            ahead(ty).wait_send()

        @pl.when(n + WINDOW < 8)
        def _():
            start_parts(part_of(n + WINDOW))

        @pl.when(jnp.logical_and(has_next, n == 8 - WINDOW))
        def _():
            start_far(False, (2,))

        @pl.when(jnp.logical_and(jnp.logical_not(has_next), n == 8 - WINDOW))
        def _():
            start_far(False)

        @pl.when(jnp.logical_and(has_next, n < 8))
        def _():
            top = pl.multiple_of(ty * TILE, TILE)
            blocks = score_rows(
                lambda c: later[c, pl.ds(top, TILE), :],
                lambda c: own[1, 8 + c : 12 + c, pl.ds(top, 64), :].reshape(256, 256),
                [later_cs[0, ty * 8 + t] for t in range(8)],
                [later_cs[1, ty * 8 + t] for t in range(8)],
                left, right, 8,
            )
            for a in range(3):
                acc_later[a, pl.ds(pl.multiple_of(ty * 8, 8), 8), :] = blocks[a]

        return 0

    lax.fori_loop(0, 9, remote_row, 0)

    mine = gather_offsets(acc)
    q_send[...] = mine
    q_slots[j] = mine

    def share(turn):
        return remote(q_send, q_slots.at[j], d_s.at[turn], d_r.at[turn], at(k, i, lax.rem(j + turn, chans)))

    for turn in range(1, chans):
        share(turn).start()

    @pl.when(has_next)
    def _():
        start_far(False, (0, 1))

    for turn in range(chans):
        if turn:
            share(turn).wait_recv()

        @pl.when(has_prev)
        def _():
            give(turn).wait_recv()

    total = jnp.zeros((16, 128), F32)
    for chan in range(chans):
        total = total + q_slots[chan]
    for chan in range(chans):
        total = total + jnp.where(has_prev, b_slots[chan], 0.0)
    scores = total * (1.0 / math.sqrt(C * TILE * TILE))
    row = lax.broadcasted_iota(jnp.int32, (16, 128), 0)
    weights = jnp.where(row < 9, 1.0 / (1.0 + jnp.exp(-scores)), 0.0)
    weight_total = jnp.sum(weights, axis=0, keepdims=True)
    fine_row = jnp.sum(weights * (row // 3 - 1).astype(F32), axis=0, keepdims=True) / weight_total
    fine_col = jnp.sum(weights * (row % 3 - 1).astype(F32), axis=0, keepdims=True) / weight_total
    lane = lax.broadcasted_iota(jnp.int32, (8, 128), 1)
    comp = lax.broadcasted_iota(jnp.int32, (8, 128), 0)
    moved = cv[...].astype(F32)
    pair = jnp.where(comp == 0, moved[0:1] + fine_row, moved[1:2] + fine_col)
    pair = jnp.where(jnp.logical_and(comp < 2, jnp.logical_or(has_prev, lane >= 64)), pair, 0.0)
    e_send[...] = pair
    e_slots[k * 3 + 1] = pair

    def tell(ahead_by, side):
        slot = k * 3 + 1 - side
        return remote(
            e_send, e_slots.at[slot], e_s.at[ahead_by, side + 1], e_r.at[slot],
            at(lax.rem(k + ahead_by, secs), lax.rem(i + side + areas, areas), j),
        )

    sides = ((-1, has_up), (0, True), (1, has_down))
    messages = [
        (ahead_by, side, jnp.logical_and(there, k + ahead_by < secs))
        for ahead_by in range(secs)
        for side, there in sides
        if ahead_by or side
    ]
    for ahead_by, side, fits in messages:

        @pl.when(fits)
        def _():
            tell(ahead_by, side).start()

    @pl.when(has_next)
    def _():
        start_far(False, (3, 4, 5))

    def hear(sec, side):
        return remote(
            e_send, e_slots.at[sec * 3 + 1 + side], e_s.at[0, 0], e_r.at[sec * 3 + 1 + side], at(prv, i, j)
        )

    for sec in range(secs):
        for side, there in sides:
            fits = jnp.logical_and(there, sec <= k if side else sec < k)

            @pl.when(fits)
            def _():
                hear(sec, side).wait_recv()

    roll = lambda x, by: pltpu.roll(x, by, 1)
    fields = []
    for side, there in sides:
        earlier = jnp.zeros((8, 128), F32)
        for sec in range(secs - 1):
            earlier = earlier + jnp.where(sec < k, e_slots[sec * 3 + 1 + side], 0.0)
        here = e_slots[k * 3 + 1 + side]
        summed = here + jnp.where(lane >= 64, roll(here, 64), 0.0) + (earlier + roll(earlier, 64))
        fields.append(jnp.where(there, summed, 0.0) if side else summed)
    tile_row, tile_col = lane % 64 // 8, lane % 8
    outside = (has_up, True, has_down)
    for sweep in range(SMOOTH):
        new = []
        for n in range(3):
            x = fields[n]
            north = roll(x, 8)
            south = roll(x, 120)
            if n > 0:
                north = jnp.where(tile_row == 0, roll(fields[n - 1], 72), north)
            if n < 2:
                south = jnp.where(tile_row == 7, roll(fields[n + 1], 56), south)
            west = jnp.where(tile_col > 0, roll(x, 1), 0.0)
            east = jnp.where(tile_col < 7, roll(x, 127), 0.0)
            grid_row = (i + n - 1) * 8 + tile_row
            count = (
                (grid_row > 0).astype(F32)
                + (grid_row < areas * 8 - 1).astype(F32)
                + (tile_col > 0).astype(F32)
                + (tile_col < 7).astype(F32)
            )
            north = jnp.where(grid_row > 0, north, 0.0)
            south = jnp.where(grid_row < areas * 8 - 1, south, 0.0)
            mean = (x + (north + south + west + east)) / (1.0 + count)
            new.append(mean if n == 1 else jnp.where(outside[n], mean, 0.0))
        fields = new
    field = fields[1]
    floors = jnp.floor(field)
    field_out[...] = field[0:2]
    whole_out[...] = floors[0:2].astype(jnp.int32)
    frac_out[...] = (field - floors)[0:2]

    for turn in range(chans):
        if turn:
            share(turn).wait_send()

        @pl.when(has_next)
        def _():
            give(turn).wait_send()

    for ahead_by, side, fits in messages:

        @pl.when(fits)
        def _():
            tell(ahead_by, side).wait_send()

    for s in range(2):

        @pl.when(has_down)
        def _():
            near_down(s).wait_send()

        @pl.when(has_up)
        def _():
            near_up(s).wait_send()

    @pl.when(has_prev)
    def _():
        coarse_back.wait_send()

    @pl.when(jnp.logical_and(has_prev, has_down))
    def _():
        relay_down.wait_send()

    @pl.when(jnp.logical_and(has_prev, has_up))
    def _():
        relay_up.wait_send()

    for n, (_, _, _, first) in enumerate(far_parts):

        @pl.when(jnp.logical_and(has_down, k >= first))
        def _():
            far_down(n).wait_send()
            far_up(n).wait_recv()

        @pl.when(jnp.logical_and(has_up, k >= first))
        def _():
            far_up(n).wait_send()
            far_down(n).wait_recv()

    for keep in keeps:
        keep.wait()


def drift_local(devices, coarse, features):
    vm = pl.BlockSpec(memory_space=pltpu.VMEM)
    sm = pl.BlockSpec(memory_space=pltpu.SMEM)
    hbm = pl.BlockSpec(memory_space=pl.ANY)
    dma = pltpu.SemaphoreType.DMA
    small = jax.ShapeDtypeStruct((2, 128), F32)
    halo = jax.ShapeDtypeStruct((2, 16, HALO, 256), BF)
    secs, areas, chans = devices
    return pl.pallas_call(
        functools.partial(drift_kernel, devices),
        out_shape=(small, jax.ShapeDtypeStruct((2, 128), jnp.int32), small, halo, halo),
        in_specs=[sm, vm, hbm],
        out_specs=(vm, vm, vm, hbm, hbm),
        scratch_shapes=[
            pltpu.VMEM((2, 16, 256 + 2 * NEAR, 256), BF),
            pltpu.VMEM((8, 256 + 2 * NEAR, 256), BF),
            pltpu.VMEM((8, 256, 256), BF),
            pltpu.VMEM((2, 128), jnp.int32),
            pltpu.VMEM((2, 128), jnp.int32),
            pltpu.SMEM((2, 128), jnp.int32),
            pltpu.VMEM((2, 128, 2048), BF),
            pltpu.VMEM((2, 192, 2048), BF),
            pltpu.VMEM((3, 2, 128, 1024), BF),
            pltpu.VMEM((3, 2, 192, 1024), BF),
            pltpu.VMEM((3, 128, 192), F32),
            pltpu.VMEM((3, 128, 192), F32),
            pltpu.VMEM((16, 128), F32),
            pltpu.VMEM((16, 128), F32),
            pltpu.VMEM((chans, 16, 128), F32),
            pltpu.VMEM((chans, 16, 128), F32),
            pltpu.VMEM((8, 128), F32),
            pltpu.VMEM((3 * secs, 8, 128), F32),
            dma((2,)), dma((2, 2)), dma((2, 2)), dma((2, 6)), dma((2, 6)), dma((2,)), dma((2,)), dma, dma, dma,
            dma((8,)), dma((8,)), dma((8,)), dma((8,)),
            dma((chans,)), dma((chans,)), dma((chans,)), dma((chans,)),
            dma((secs, 3)), dma((3 * secs,)), dma((2, 2)),
        ],
        compiler_params=pltpu.CompilerParams(
            collective_id=0, has_side_effects=True, vmem_limit_bytes=48 * 2**20
        ),
        name="drift",
    )(coarse, coarse, features)


def warp_kernel(
    areas, whole, frac, field, feat, top_halo, bottom_halo, out_ref, field_out, held, rows_all, sems
):
    step = pl.program_id(0)
    s = step // 4
    ty0 = step % 4 * 2
    i = lax.axis_index("area")

    def load(section, part):
        if part == 0:
            halo, there = top_halo, pl.ds(0, HALO)
        else:
            halo, there = bottom_halo, pl.ds(HALO + 256, HALO)
        return [
            pltpu.make_async_copy(
                feat.at[section, :, pl.ds(128 * part, 128), :],
                held.at[section, :, pl.ds(HALO + 128 * part, 128), :],
                sems.at[section, part, 0],
            ),
            pltpu.make_async_copy(halo.at[section], held.at[section, :, there, :], sems.at[section, part, 1]),
        ]

    def start(section, part):
        for copy in load(section, part):
            copy.start()

    def wait(section, part):
        for copy in load(section, part):
            copy.wait()

        @pl.when(i == (0 if part == 0 else areas - 1))
        def _():
            held[section, :, pl.ds(0 if part == 0 else HALO + 256, HALO), :] = jnp.zeros((16, HALO, 256), BF)

    @pl.when(step == 0)
    def _():
        start(0, 0)
        start(0, 1)
        lane = lax.broadcasted_iota(jnp.int32, (32, 128), 1)
        row = lax.broadcasted_iota(jnp.int32, (32, 128), 0)
        spread = jnp.where(row < 16, field[0:1, :], field[1:2, :])
        spread = jnp.where(lane // 8 == row % 16, spread, 0.0)
        pick = lax.broadcasted_iota(jnp.int32, (128, 8), 0) % 8 == lax.broadcasted_iota(jnp.int32, (128, 8), 1)
        grid = jnp.dot(
            spread, pick.astype(F32), precision=lax.Precision.HIGHEST, preferred_element_type=F32
        )
        field_out[...] = grid.reshape(2, 2, 8, 8)
        wait(0, 0)

    @pl.when(step == 1)
    def _():
        start(1, 0)
        start(1, 1)
        wait(0, 1)

    @pl.when(step == 4)
    def _():
        wait(1, 0)
        wait(1, 1)

    lane = lax.broadcasted_iota(jnp.int32, (1, 128), 1)
    lane_tile = lane // TILE
    src_col = lax.broadcasted_iota(jnp.int32, (256, 128), 0)
    parts = []
    need = jnp.int32(0)
    for q in range(2):
        base = HALO + TILE * (ty0 + q)
        for h in range(2):
            at = s * 64 + (ty0 + q) * 8 + 4 * h
            fl_row = [whole[0, at + t] for t in range(4)]
            low = jnp.minimum(jnp.minimum(fl_row[0], fl_row[1]), jnp.minimum(fl_row[2], fl_row[3]))
            high = jnp.maximum(jnp.maximum(fl_row[0], fl_row[1]), jnp.maximum(fl_row[2], fl_row[3]))
            full = (base + low) // 16 * 16
            need = jnp.maximum(need, (base + high + TILE + 1 - full + 15) // 16)
            parts.append((q, h, at, base, fl_row, full))
    loaded = jnp.where(jnp.logical_and(s == 0, ty0 < 2), 192, 2 * HALO + 256)

    def run(n):
        for q, h, at, base, fl_row, full in parts:
            rows = rows_all.at[2 * q + h]
            fl_col = [whole[1, at + t] for t in range(4)]
            fr_row = lane_pick([frac[0, at + t] for t in range(4)], lane_tile)
            fr_col = lane_pick([frac[1, at + t] for t in range(4)], lane_tile)
            rel = src_col - (lane + 128 * h + lane_pick(fl_col, lane_tile))
            weight = jnp.where(rel == 0, 1.0 - fr_col, jnp.where(rel == 1, fr_col, 0.0))
            coarse_part = weight.astype(BF)
            fine_part = (weight - coarse_part.astype(F32)).astype(BF)
            mixer = jnp.concatenate([coarse_part, fine_part], 1)
            start = pl.multiple_of(jnp.minimum(full, loaded - 16 * n), 16)
            block = held[s, :, pl.ds(start, 16 * n), :].reshape(256 * n, 256)
            mixed = jnp.dot(block, mixer, preferred_element_type=F32)
            mixed = mixed[:, :128] + mixed[:, 128:]
            rows[:, 0 : 16 * n, :] = mixed.reshape(16, 16 * n, 128)
            between = [jnp.logical_and(lane_tile == t, fr_row > 0.0) for t in range(4)]
            offs = [base + fl_row[t] - start for t in range(4)]
            for c in range(16):
                upper = rows[c, pl.ds(offs[0], TILE), :]
                lower = jnp.where(between[0], rows[c, pl.ds(offs[0] + 1, TILE), :], 0.0)
                for t in range(1, 4):
                    upper = jnp.where(lane_tile == t, rows[c, pl.ds(offs[t], TILE), :], upper)
                    lower = jnp.where(between[t], rows[c, pl.ds(offs[t] + 1, TILE), :], lower)
                out_ref[0, c, TILE * q : TILE * q + TILE, 128 * h : 128 * h + 128] = (
                    (1.0 - fr_row) * upper + fr_row * lower
                ).astype(BF)

    least = 0
    for n in (4, 6, 8, 10):
        pl.when(jnp.logical_and(need > least, need <= n))(functools.partial(run, n))
        least = n


def warp_local(areas, whole, frac, field, features, top_halo, bottom_halo):
    sm = pl.BlockSpec(memory_space=pltpu.SMEM)
    hbm = pl.BlockSpec(memory_space=pl.ANY)
    return pl.pallas_call(
        functools.partial(warp_kernel, areas),
        grid=(8,),
        out_shape=(
            jax.ShapeDtypeStruct((2, 16, 256, 256), BF),
            jax.ShapeDtypeStruct((2, 2, 8, 8), F32),
        ),
        in_specs=[sm, sm, pl.BlockSpec(memory_space=pltpu.VMEM), hbm, hbm, hbm],
        out_specs=(
            pl.BlockSpec((1, 16, 2 * TILE, 256), lambda g: (g // 4, 0, g % 4, 0)),
            pl.BlockSpec(memory_space=pltpu.VMEM),
        ),
        scratch_shapes=[
            pltpu.VMEM((2, 16, 2 * HALO + 256, 256), BF),
            pltpu.VMEM((4, 16, 160, 128), F32),
            pltpu.SemaphoreType.DMA((2, 2, 2)),
        ],
        compiler_params=pltpu.CompilerParams(vmem_limit_bytes=24 * 2**20),
        name="warp",
    )(whole, frac, field, features, top_halo, bottom_halo)


def local(devices, features, coarse):
    field, whole, frac, top_halo, bottom_halo = drift_local(devices, coarse, features)
    return warp_local(devices[1], whole, frac, field, features, top_halo, bottom_halo)


def solution(mesh):
    placed = (P("sec", "chan", "area", None), P(None, "sec", "area", None))
    devices = tuple(mesh.shape[name] for name in ("sec", "area", "chan"))
    return jax.shard_map(
        functools.partial(local, devices),
        mesh=mesh,
        in_specs=placed,
        out_specs=placed,
        check_vma=False,
    )
```
